256 devices in a mesh: win: 8 (over y, z_lo), rcv: 32 (over x, z_hi, core).
Axes of the slice: x: 4, y: 4, z: 8 (z_hi: 4, z_lo: 2; z = z_hi * 2 + z_lo), core: 2. Of those that a mesh axis runs over, the one named last changes fastest.
Arguments:
- source_spectra: bfloat16 [256, 4096, 1024], P('win', 'rcv'), may hold values from -6 to 6
- receiver_spectra: bfloat16 [256, 512, 1024], P('win', 'rcv'), may hold values from -6 to 6
- source_block: int32 [1], replicated, may hold values from 0 to 31
- bad_channels: int32 [64], replicated, may hold values from 0 to 511
Outputs:
- correlations: float32 [128, 512, 1024], P('win', 'rcv')
The draws below stay inside these ranges and needn't reach their ends.
Inputs may be any that keep to these rules, and one draw needn't show every extreme that they name: `source_block`: the rcv index of the device that holds the block. `bad_channels`: repeats may occur.
All inputs are finite; a program needn't handle non-finite values.
Results may differ from the reference program's by a relative error of at most 0.0036.
Values may be sent and summed in bfloat16 or wider, within the bound.
No kernel may reach another device: no remote copies, remote signals or barrier semaphores. Data moves between devices by JAX's collectives and lax.ppermute only.
A program may use at most 128 MiB of HBM per device.

```python
import math
import jax
import jax.numpy as jnp
from jax import lax

LAGS = 1024
SRC = 128
WINDOWS = 256
CHANNELS = 512
SOURCES = 4096
BAD = 64
N_RCV = 32


def plant(values, key, least, top_value):
    dims = values.shape
    index_at = [jax.random.randint(jax.random.fold_in(key, axis), (), 0, dims[axis]) for axis in range(len(dims))]
    values = values.at[tuple(index_at)].set(least)
    longest = dims.index(max(dims))
    index_at[longest] = (index_at[longest] + 1) % dims[longest]
    return values.at[tuple(index_at)].set(top_value)


def block_scale(rng, dims, pieces, smallest, top_value):
    gain = 1.0
    for dim, shards_of in pieces:
        draws = jax.random.uniform(jax.random.fold_in(jax.random.fold_in(rng, 6), dim), (shards_of,), jnp.float32, smallest / len(pieces), top_value / len(pieces))
        gain = gain * jnp.repeat(jnp.exp(draws), dims[dim] // shards_of).reshape((-1,) + (1,) * (len(dims) - 1 - dim))
    return gain


def scatter_about(stream_key, shape, spread, bound, pieces=(), kind=jnp.bfloat16):
    values = spread * jax.random.normal(stream_key, shape, jnp.float32)
    if pieces:
        values = values * block_scale(stream_key, shape, pieces, -0.22, 0.18)
    return jnp.clip(values, -bound, bound).astype(kind)


def setup_inputs(seed: int = 0) -> dict:
    keys = jax.random.split(jax.random.key(seed), 5)
    return {
        "source_spectra": scatter_about(keys[0], (WINDOWS, SOURCES, LAGS), 1.0, 6.0, ((0, 8), (1, 32))),
        "receiver_spectra": scatter_about(keys[1], (WINDOWS, CHANNELS, LAGS), 1.0, 6.0, ((0, 8), (1, 32))),
        "source_block": jax.random.randint(keys[2], (1,), 0, N_RCV).astype(jnp.int32),
        "bad_channels": plant(jax.random.randint(keys[3], (BAD,), 0, CHANNELS), jax.random.fold_in(keys[3], 1), 0, CHANNELS - 1).astype(jnp.int32),
    }


def whiten(spectra):
    half = spectra.shape[-1] // 2
    real_part = spectra[..., :half]
    imag_part = spectra[..., half:]
    power = real_part * real_part + imag_part * imag_part
    level = lax.optimization_barrier(jnp.mean(power, axis=-1, keepdims=True))
    factor = lax.rsqrt(power + 0.1 * level + 1e-06)
    return jnp.concatenate([real_part * factor, imag_part * factor], axis=-1)

def inverse_table(lags, windows):
    half = lags // 2
    freq = jnp.arange(half, dtype=jnp.int32)[:, None]
    lag_index = jnp.arange(lags, dtype=jnp.int32)[None, :]
    phase = (freq * lag_index % lags).astype(jnp.float32) * (2.0 * math.pi / lags)
    weight = jnp.where(freq == 0, 1.0, 2.0).astype(jnp.float32) / jnp.sqrt(jnp.float32(windows * lags))
    return jnp.concatenate([weight * jnp.cos(phase), -weight * jnp.sin(phase)], axis=0)

def reference(source_spectra, receiver_spectra, source_block, bad_channels):
    half = LAGS // 2
    start = (source_block[0] * SRC).astype(jnp.int32)
    block = lax.dynamic_slice_in_dim(source_spectra, start, SRC, 1)
    src_white = whiten(block.astype(jnp.float32)).astype(jnp.bfloat16)
    channel_ids = jnp.arange(CHANNELS, dtype=jnp.int32)
    faulty = jnp.any(bad_channels[:, None] == channel_ids[None, :], axis=0)
    keep = jnp.where(faulty, 0.0, 1.0).astype(jnp.float32)
    rcv_white = (whiten(receiver_spectra.astype(jnp.float32)) * keep[None, :, None]).astype(jnp.bfloat16)
    src_wide = src_white.astype(jnp.float32)
    rcv_wide = rcv_white.astype(jnp.float32)
    high = lax.Precision.HIGHEST
    s_re, s_im = (src_wide[..., :half], src_wide[..., half:])
    r_re, r_im = (rcv_wide[..., :half], rcv_wide[..., half:])
    cross_re = jnp.einsum('wsf,wcf->scf', s_re, r_re, precision=high) + jnp.einsum('wsf,wcf->scf', s_im, r_im, precision=high)
    cross_im = jnp.einsum('wsf,wcf->scf', s_re, r_im, precision=high) - jnp.einsum('wsf,wcf->scf', s_im, r_re, precision=high)
    cross = jnp.concatenate([cross_re, cross_im], axis=-1)
    table = inverse_table(LAGS, WINDOWS)
    flat = cross.reshape(SRC * CHANNELS, LAGS)
    result = jnp.dot(flat, table, precision=high, preferred_element_type=jnp.float32)
    return result.reshape(SRC, CHANNELS, LAGS)
```

```python
import functools
import math

import jax
import jax.numpy as jnp
import numpy as np
from jax import lax
from jax.experimental import pallas as pl
from jax.experimental.pallas import tpu as pltpu
from jax.sharding import Mesh
from jax.sharding import PartitionSpec as P

AXES = ("y", "zl", "x", "zh", "core")
SIZES = (4, 2, 4, 4, 2)
LAGS = 1024
HALF = 512
WINDOWS = 256
VMEM = 48 * 1024 * 1024


def whiten_parts(re, im):
    power = re * re + im * im
    level = jnp.mean(power, axis=-1, keepdims=True)
    factor = lax.rsqrt(power + 0.1 * level + 1e-06)
    return re * factor, im * factor


def source_kernel(place, src_ref, *refs):
    outs, held = refs[:8], refs[8]
    core, x = place[0], place[1]
    block = src_ref.shape[0]
    data = src_ref[...].astype(jnp.float32)
    re, im = whiten_parts(data[..., :HALF], data[..., HALF:])
    for k in range(2):
        half_re = jnp.concatenate(
            [re[:, w * 16 + k * 8 : w * 16 + k * 8 + 8] for w in range(8)], axis=1
        )
        half_im = jnp.concatenate(
            [im[:, w * 16 + k * 8 : w * 16 + k * 8 + 8] for w in range(8)], axis=1
        )
        for q in range(4):
            lanes = slice(q * 128, q * 128 + 128)
            held[k * 4 + q, :, :, :128] = half_re[..., lanes].astype(jnp.bfloat16)
            held[k * 4 + q, :, :, 128:] = half_im[..., lanes].astype(jnp.bfloat16)
    for j in range(2):
        k = core if j == 0 else 1 - core
        for r in range(4):
            outs[j * 4 + r][...] = held[k * 4 + lax.rem(x + r, 4)]


def source_pieces(src, core, x):
    windows, sources, _ = src.shape
    block = 4
    place = jnp.stack([core, x]).astype(jnp.int32)
    piece = jax.ShapeDtypeStruct((windows, 64, 256), jnp.bfloat16)
    return pl.pallas_call(
        source_kernel,
        out_shape=[piece] * 8,
        grid_spec=pltpu.PrefetchScalarGridSpec(
            num_scalar_prefetch=1,
            grid=(windows // block,),
            in_specs=[pl.BlockSpec((block, sources, LAGS), lambda i, p: (i, 0, 0))],
            out_specs=[pl.BlockSpec((block, 64, 256), lambda i, p: (i, 0, 0))] * 8,
            scratch_shapes=[pltpu.VMEM((8, block, 64, 256), jnp.bfloat16)],
        ),
        compiler_params=pltpu.CompilerParams(vmem_limit_bytes=VMEM),
        cost_estimate=pl.CostEstimate(
            flops=40_000_000, bytes_accessed=16 * 2**20, transcendentals=2_000_000
        ),
    )(place, src)


def cross_kernel(src_ref, rcv_ref, out_ref, acc):
    lane = lax.broadcasted_iota(jnp.int32, (128, 128), 1)
    is_real = lax.rem(lane, 64) < 32
    first = lane < 64
    for win in range(8):
        plain = src_ref[win].astype(jnp.float32)
        turned = jnp.where(
            is_real, -pltpu.roll(plain, 96, axis=1), pltpu.roll(plain, 32, axis=1)
        )
        rows = jnp.concatenate(
            [
                jnp.where(first, plain, 0.0),
                jnp.where(first, turned, 0.0),
                jnp.where(first, 0.0, plain),
                jnp.where(first, 0.0, turned),
            ],
            axis=0,
        ).astype(jnp.bfloat16)
        part = lax.dot_general(
            rows, rcv_ref[win], (((1,), (1,)), ((), ())), preferred_element_type=jnp.float32
        )
        if win == 0:
            acc[...] = part
        else:
            acc[...] += part
    group = lax.broadcasted_iota(jnp.int32, (64, 128), 1) // 16
    for v in range(4):
        cols = slice(v * 128, v * 128 + 128)
        held = [
            jnp.concatenate(
                [acc[b * 64 + s * 8 : b * 64 + s * 8 + 8, cols] for b in range(8)], axis=0
            )
            for s in range(8)
        ]
        for bit in (4, 2, 1):
            low = (group & bit) == 0
            for s in range(8):
                if s & bit:
                    continue
                a, b = held[s], held[s + bit]
                held[s] = jnp.where(low, a, pltpu.roll(b, 16 * bit, axis=1))
                held[s + bit] = jnp.where(low, pltpu.roll(a, 128 - 16 * bit, axis=1), b)
        for g in range(0, 8, 2):
            row = (v * 8 + g) * 8
            for b in range(8):
                pair = jnp.concatenate(
                    [held[g][b * 8 : b * 8 + 8], held[g + 1][b * 8 : b * 8 + 8]], axis=0
                )
                out_ref[row : row + 16, b * 128 : b * 128 + 128] = pair.astype(jnp.bfloat16)


def cross_sums(src, rcv):
    return pl.pallas_call(
        cross_kernel,
        out_shape=jax.ShapeDtypeStruct((256, 1024), jnp.bfloat16),
        in_specs=[pl.BlockSpec(memory_space=pltpu.VMEM)] * 2,
        out_specs=pl.BlockSpec(memory_space=pltpu.VMEM),
        scratch_shapes=[pltpu.VMEM((512, 512), jnp.float32)],
        compiler_params=pltpu.CompilerParams(vmem_limit_bytes=VMEM),
    )(src, rcv)


def lag_kernel(cross_ref, high_ref, low_ref, out_ref):
    total = None
    for b in range(4):
        rows = cross_ref[:, b * 256 : b * 256 + 256]
        for table in (high_ref, low_ref):
            part = lax.dot_general(
                rows,
                table[b * 256 : b * 256 + 256, :],
                (((0,), (0,)), ((), ())),
                preferred_element_type=jnp.float32,
            )
            total = part if total is None else total + part
    out_ref[...] = total


def to_lags(cross, high, low):
    return pl.pallas_call(
        lag_kernel,
        out_shape=jax.ShapeDtypeStruct((256, LAGS), jnp.float32),
        grid=(4,),
        in_specs=[
            pl.BlockSpec((256, 1024), lambda i: (0, 0)),
            pl.BlockSpec((1024, 256), lambda i: (0, i)),
            pl.BlockSpec((1024, 256), lambda i: (0, i)),
        ],
        out_specs=pl.BlockSpec((256, 256), lambda i: (0, i)),
        compiler_params=pltpu.CompilerParams(vmem_limit_bytes=VMEM),
    )(cross, high, low)


def inverse_table():
    x, zh, core, win = np.meshgrid(
        np.arange(4), np.arange(4), np.arange(2), np.arange(8), indexing="ij"
    )
    place = (x * 128 + (win * 4 + zh) * 2 + core).reshape(-1)
    lag = np.arange(LAGS)
    rows = []
    for j in range(2):
        freq = place + 64 * j
        phase = (freq[:, None] * lag[None, :] % LAGS) * (2.0 * math.pi / LAGS)
        weight = np.where(freq == 0, 1.0, 2.0)[:, None] / math.sqrt(WINDOWS * LAGS)
        rows += [weight * np.cos(phase), -weight * np.sin(phase)]
    table = np.concatenate(rows, axis=0)
    high = jnp.asarray(table, jnp.float32).astype(jnp.bfloat16)
    low = (jnp.asarray(table, jnp.float32) - high.astype(jnp.float32)).astype(jnp.bfloat16)
    return high, low


def on_device(source_spectra, receiver_spectra, source_block, bad_channels):
    win_local, chans, _ = receiver_spectra.shape
    x, zh, core = (lax.axis_index(a) for a in ("x", "zh", "core"))
    holder = source_block[0]
    hx, hz, hc = holder // 8, (holder // 2) % 4, holder % 2

    channel_ids = ((x * 4 + zh) * 2 + core) * chans + jnp.arange(chans, dtype=jnp.int32)
    faulty = jnp.any(bad_channels[:, None] == channel_ids[None, :], axis=0)
    keep = jnp.where(faulty, 0.0, 1.0).astype(jnp.float32)[None, :, None]
    wide = receiver_spectra.astype(jnp.float32)
    r_re, r_im = whiten_parts(wide[..., :HALF], wide[..., HALF:])
    white = jnp.stack([r_re * keep, r_im * keep], axis=2).astype(jnp.bfloat16)
    blocks = white.reshape(win_local, chans, 2, 4, 2, 8, 8).transpose(5, 3, 6, 1, 4, 2, 0)
    blocks = blocks.reshape(256, chans, 128)
    rcv_at = lax.all_to_all(blocks, AXES, 0, 0, tiled=True).reshape(8, 512, 128)

    pieces = source_pieces(source_spectra, core, x)
    swap = [(0, 1), (1, 0)]
    up = [(i, (i + 1) % 4) for i in range(4)]
    down = [(i, (i + 3) % 4) for i in range(4)]
    half = {}
    for r in (2, 1, 3, 0):
        other = lax.ppermute(pieces[4 + r], "core", swap)
        half[r] = jnp.where(core == hc, pieces[r], other)
    mid = win_local // 2
    far_up = lax.ppermute(half[2][:mid], "x", up)
    far_down = lax.ppermute(half[2][mid:], "x", down)
    near_up = lax.ppermute(half[1], "x", up)
    near_down = lax.ppermute(half[3], "x", down)
    far_up = lax.ppermute(far_up, "x", up)
    far_down = lax.ppermute(far_down, "x", down)
    away = (x - hx) % 4
    far = jnp.concatenate([far_up, far_down], axis=0)
    quarter = jnp.where(
        away == 0,
        half[0],
        jnp.where(away == 1, near_up, jnp.where(away == 2, far, near_down)),
    )
    blocks = quarter.reshape(win_local, 8, 8, 2, 2, 64).transpose(5, 2, 1, 4, 3, 0)
    blocks = blocks.reshape(64, 64, 128)
    got = lax.all_to_all(blocks, ("y", "zl", "zh", "core"), 0, 0, tiled=True)
    got = lax.dynamic_index_in_dim(got.reshape(8, 4, 2, 64, 128), hz, 1, keepdims=False)
    src_at = got.reshape(8, 128, 128)

    sums = cross_sums(src_at, rcv_at)
    mine = lax.all_to_all(sums, ("x", "zh", "core", "y", "zl"), 0, 0, tiled=True)
    high, low = inverse_table()
    return to_lags(mine, high, low).reshape(16, 16, LAGS)


def solution(mesh):
    fine = Mesh(mesh.devices.reshape(SIZES), AXES)
    win, rcv = AXES[:2], AXES[2:]
    return jax.shard_map(
        on_device,
        mesh=fine,
        in_specs=(P(win, rcv, None), P(win, rcv, None), P(), P()),
        out_specs=P(win, rcv, None),
        check_vma=False,
    )
```

```python
import functools
import math

import jax
import jax.numpy as jnp
import numpy as np
from jax import lax
from jax.experimental import pallas as pl
from jax.experimental.pallas import tpu as pltpu
from jax.sharding import Mesh
from jax.sharding import PartitionSpec as P

AXES = ("y", "zl", "x", "zh", "core")
SIZES = (4, 2, 4, 4, 2)
LAGS = 1024
HALF = 512
WINDOWS = 256
VMEM = 60 * 1024 * 1024
BF16 = jnp.bfloat16
F32 = jnp.float32


def whiten_parts(re, im, keep=None):
    power = re * re + im * im
    level = jnp.mean(power, axis=-1, keepdims=True)
    factor = lax.rsqrt(power + 0.1 * level + 1e-06)
    if keep is not None:
        factor = factor * keep
    return re * factor, im * factor


def source_kernel(place, src_ref, far_low, far_high, up, down, own, held):
    x = place[0]
    step, steps = pl.program_id(0), pl.num_programs(0)
    data = src_ref[...].astype(F32)
    re, im = (
        jnp.concatenate(
            [part[:, w * 16 + k * 8 : w * 16 + k * 8 + 8] for k in range(2) for w in range(8)],
            axis=1,
        )
        for part in whiten_parts(data[..., :HALF], data[..., HALF:])
    )
    for q in range(4):
        lanes = slice(q * 128, q * 128 + 128)
        held[q, :, :, :128] = re[..., lanes].astype(BF16)
        held[q, :, :, 128:] = im[..., lanes].astype(BF16)
    own[...] = held[x]
    up[...] = held[lax.rem(x + 1, 4)]
    down[...] = held[lax.rem(x + 3, 4)]

    @pl.when(step < steps // 2)
    def _():
        far_low[...] = held[lax.rem(x + 2, 4)]

    @pl.when(step >= steps // 2)
    def _():
        far_high[...] = held[lax.rem(x + 2, 4)]


def source_pieces(src, place):
    windows, sources, _ = src.shape
    block = 4
    steps = windows // block
    part = jax.ShapeDtypeStruct((windows // 2, sources, 256), BF16)
    piece = jax.ShapeDtypeStruct((windows, sources, 256), BF16)
    shape = (block, sources, 256)
    low = pl.BlockSpec(shape, lambda i, p: (jnp.minimum(i, steps // 2 - 1), 0, 0))
    high = pl.BlockSpec(shape, lambda i, p: (jnp.maximum(i - steps // 2, 0), 0, 0))
    plain = pl.BlockSpec(shape, lambda i, p: (i, 0, 0))
    return pl.pallas_call(
        source_kernel,
        out_shape=[part] * 2 + [piece] * 3,
        grid_spec=pltpu.PrefetchScalarGridSpec(
            num_scalar_prefetch=1,
            grid=(steps,),
            in_specs=[pl.BlockSpec((block, sources, LAGS), lambda i, p: (i, 0, 0))],
            out_specs=[low, high] + [plain] * 3,
            scratch_shapes=[pltpu.VMEM((4,) + shape, BF16)],
        ),
        compiler_params=pltpu.CompilerParams(vmem_limit_bytes=VMEM),
        cost_estimate=pl.CostEstimate(
            flops=40_000_000, bytes_accessed=16 * 2**20, transcendentals=2_000_000
        ),
    )(place, src)


def turn_pair(*parts):
    tall = jnp.concatenate(parts, axis=0).T
    low = lax.broadcasted_iota(jnp.int32, (64, 128), 1) < 64
    top, bottom = tall[:64], tall[64:]
    return (
        jnp.where(low, top, pltpu.roll(bottom, 64, axis=1)),
        jnp.where(low, pltpu.roll(top, 64, axis=1), bottom),
    )


def receiver_kernel(place, bad, rcv_ref, out_ref, held, turned):
    windows, chans, _ = rcv_ref.shape
    ids = place[1] * chans + lax.broadcasted_iota(jnp.int32, (chans, 128), 0)
    faulty = ids < 0
    for i in range(bad.shape[0]):
        faulty = faulty | (ids == bad[i])
    keep = jnp.where(faulty, 0.0, 1.0).astype(F32)[None, :, :1]
    data = rcv_ref[...].astype(F32)
    re, im = whiten_parts(data[..., :HALF], data[..., HALF:], keep)
    for q in range(4):
        lanes = slice(q * 128, q * 128 + 128)
        held[2 * q] = re[..., lanes].reshape(windows * chans, 128)
        held[2 * q + 1] = im[..., lanes].reshape(windows * chans, 128)
    for q in range(4):
        for c in range(0, chans, 2):
            pair = turn_pair(
                *(
                    held[2 * q + part, pl.ds(c + i, windows, stride=chans), :]
                    for i in range(2)
                    for part in range(2)
                )
            )
            for i in range(2):
                turned[pl.ds(q * 64 * chans + c + i, 64, stride=chans), :] = pair[i]
    out_ref[...] = turned[...].reshape(256, chans, 128).astype(BF16)


def receiver_blocks(rcv, place, bad):
    windows, chans, _ = rcv.shape
    return pl.pallas_call(
        receiver_kernel,
        out_shape=jax.ShapeDtypeStruct((256, chans, 128), BF16),
        grid_spec=pltpu.PrefetchScalarGridSpec(
            num_scalar_prefetch=2,
            grid=(1,),
            in_specs=[pl.BlockSpec(rcv.shape, lambda i, p, b: (0, 0, 0))],
            out_specs=pl.BlockSpec((256, chans, 128), lambda i, p, b: (0, 0, 0)),
            scratch_shapes=[
                pltpu.VMEM((8, windows * chans, 128), F32),
                pltpu.VMEM((256 * chans, 128), F32),
            ],
        ),
        compiler_params=pltpu.CompilerParams(vmem_limit_bytes=VMEM),
        cost_estimate=pl.CostEstimate(
            flops=20_000_000, bytes_accessed=2 * 2**20, transcendentals=300_000
        ),
    )(place, bad, rcv)


def take(away, pieces, core, target, sem):
    windows = target.shape[0]
    far_low, far_high, up, down, own = (ref.at[:, pl.ds(core * 64, 64)] for ref in pieces)

    def fetch(pairs):
        copies = [pltpu.make_async_copy(a, b, sem.at[i]) for i, (a, b) in enumerate(pairs)]
        for copy in copies:
            copy.start()
        for copy in copies:
            copy.wait()

    mid = windows // 2
    low, high = target.at[pl.ds(0, mid)], target.at[pl.ds(mid, mid)]
    for distance, pairs in (
        (0, [(own, target)]),
        (1, [(up, target)]),
        (2, [(far_low, low), (far_high, high)]),
        (3, [(down, target)]),
    ):
        pl.when(away == distance)(functools.partial(fetch, pairs))


def share_kernel(core, place, *refs):
    take(place[3], refs[:5], core, refs[5], refs[6])


def share(core, place, pieces):
    windows = pieces[-1].shape[0]
    return pl.pallas_call(
        functools.partial(share_kernel, core),
        out_shape=jax.ShapeDtypeStruct((windows, 64, 256), BF16),
        grid_spec=pltpu.PrefetchScalarGridSpec(
            num_scalar_prefetch=1,
            grid=(1,),
            in_specs=[pl.BlockSpec(memory_space=pl.ANY)] * 5,
            out_specs=pl.BlockSpec((windows, 64, 256), lambda i, p: (0, 0, 0)),
            scratch_shapes=[pltpu.SemaphoreType.DMA((2,))],
        ),
        compiler_params=pltpu.CompilerParams(vmem_limit_bytes=VMEM),
    )(place, *pieces)


def turn_kernel(holder_core, place, *refs):
    shared, out_ref, piece, held, turned, sem = refs[5:]
    windows = piece.shape[0]

    @pl.when(place[2] == holder_core)
    def _():
        take(place[3], refs[:5], holder_core, piece, sem)

    @pl.when(place[2] != holder_core)
    def _():
        copy = pltpu.make_async_copy(shared, piece, sem.at[0])
        copy.start()
        copy.wait()

    for part in range(2):
        lanes = slice(part * 128, part * 128 + 128)
        held[part] = piece[:, :, lanes].astype(F32).reshape(windows * 64, 128)
    for row in range(0, 64, 2):
        s, w = row // 8, row % 8
        pair = turn_pair(
            *(
                held[part, pl.ds(w * 8 + i * 8 + s, windows, stride=64), :]
                for i in range(2)
                for part in range(2)
            )
        )
        for i in range(2):
            turned[pl.ds(row + i, 64, stride=64), :] = pair[i]
    out_ref[...] = turned[...].reshape(64, 64, 128).astype(BF16)


def turn_source(holder_core, place, pieces, shared):
    windows = pieces[-1].shape[0]
    return pl.pallas_call(
        functools.partial(turn_kernel, holder_core),
        out_shape=jax.ShapeDtypeStruct((64, 64, 128), BF16),
        grid_spec=pltpu.PrefetchScalarGridSpec(
            num_scalar_prefetch=1,
            grid=(1,),
            in_specs=[pl.BlockSpec(memory_space=pl.ANY)] * 6,
            out_specs=pl.BlockSpec((64, 64, 128), lambda i, p: (0, 0, 0)),
            scratch_shapes=[
                pltpu.VMEM((windows, 64, 256), BF16),
                pltpu.VMEM((2, windows * 64, 128), F32),
                pltpu.VMEM((64 * 64, 128), F32),
                pltpu.SemaphoreType.DMA((2,)),
            ],
        ),
        compiler_params=pltpu.CompilerParams(vmem_limit_bytes=VMEM),
    )(place, *pieces, shared)


def cross_kernel(place, src_ref, rcv_ref, out_ref, acc):
    row = lax.broadcasted_iota(jnp.int32, (512, 128), 0)
    col = lax.broadcasted_iota(jnp.int32, (512, 128), 1)
    spread = ((row // 8 == col % 64) & (row % 2 == col // 64)).astype(F32).astype(BF16)
    turned_row = (row // 2) % 2 == 1
    is_real = col % 64 < 32
    used = (row // 4) % 2 == col // 64
    zh = place[4]
    for win in range(8):
        base = (win * 4 + zh) * 2
        rows = jnp.concatenate([src_ref[base], src_ref[base + 1]], axis=0)
        plain = jnp.dot(spread, rows, preferred_element_type=F32)
        turned = jnp.where(
            is_real, -pltpu.roll(plain, 96, axis=1), pltpu.roll(plain, 32, axis=1)
        )
        left = jnp.where(used, jnp.where(turned_row, turned, plain), 0.0).astype(BF16)
        right = jnp.concatenate([rcv_ref[x * 8 + win] for x in range(4)], axis=0)
        part = lax.dot_general(left, right, (((1,), (1,)), ((), ())), preferred_element_type=F32)
        if win == 0:
            acc[...] = part
        else:
            acc[...] += part
    group = lax.broadcasted_iota(jnp.int32, (64, 128), 1) // 16
    for v in range(4):
        cols = slice(v * 128, v * 128 + 128)
        held = [acc[s * 64 : s * 64 + 64, cols] for s in range(8)]
        for bit in (4, 2, 1):
            low = (group & bit) == 0
            for s in range(8):
                if s & bit:
                    continue
                a, b = held[s], held[s + bit]
                held[s] = jnp.where(low, a, pltpu.roll(b, 16 * bit, axis=1))
                held[s + bit] = jnp.where(low, pltpu.roll(a, 128 - 16 * bit, axis=1), b)
        for g in range(8):
            first = (v * 8 + g) * 8
            out_ref[first : first + 8] = held[g].reshape(8, 8, 128).astype(BF16)


def cross_sums(place, src, rcv):
    return pl.pallas_call(
        cross_kernel,
        out_shape=jax.ShapeDtypeStruct((256, 8, 128), BF16),
        grid_spec=pltpu.PrefetchScalarGridSpec(
            num_scalar_prefetch=1,
            grid=(1,),
            in_specs=[
                pl.BlockSpec(src.shape, lambda i, p: (0, 0, 0)),
                pl.BlockSpec(rcv.shape, lambda i, p: (0, 0, 0)),
            ],
            out_specs=pl.BlockSpec((256, 8, 128), lambda i, p: (0, 0, 0)),
            scratch_shapes=[pltpu.VMEM((512, 512), F32)],
        ),
        compiler_params=pltpu.CompilerParams(vmem_limit_bytes=VMEM),
    )(place, src, rcv)


def lag_kernel(cross_ref, high_ref, low_ref, out_ref, wide, sorted_ref):
    @pl.when(pl.program_id(0) == 0)
    def _():
        wide[...] = cross_ref[...].astype(F32).reshape(2048, 128)
        for b in range(8):
            rows = wide[pl.ds(b, 256, stride=8), :].astype(BF16)
            sorted_ref[b // 2, :, b % 2 * 128 : b % 2 * 128 + 128] = rows

    total = None
    for b in range(4):
        for table in (high_ref, low_ref):
            part = lax.dot_general(
                sorted_ref[b],
                table[b * 256 : b * 256 + 256, :],
                (((0,), (0,)), ((), ())),
                preferred_element_type=F32,
            )
            total = part if total is None else total + part
    out_ref[...] = total


def to_lags(cross, high, low):
    return pl.pallas_call(
        lag_kernel,
        out_shape=jax.ShapeDtypeStruct((256, LAGS), F32),
        grid=(4,),
        in_specs=[
            pl.BlockSpec((256, 8, 128), lambda i: (0, 0, 0)),
            pl.BlockSpec((1024, 256), lambda i: (0, i)),
            pl.BlockSpec((1024, 256), lambda i: (0, i)),
        ],
        out_specs=pl.BlockSpec((256, 256), lambda i: (0, i)),
        scratch_shapes=[pltpu.VMEM((2048, 128), F32), pltpu.VMEM((4, 256, 256), BF16)],
        compiler_params=pltpu.CompilerParams(vmem_limit_bytes=VMEM),
    )(cross, high, low)


def inverse_table():
    x, zh, core, win = np.meshgrid(
        np.arange(4), np.arange(4), np.arange(2), np.arange(8), indexing="ij"
    )
    place = (x * 128 + (win * 4 + zh) * 2 + core).reshape(-1)
    lag = np.arange(LAGS)
    rows = []
    for j in range(2):
        freq = place + 64 * j
        phase = (freq[:, None] * lag[None, :] % LAGS) * (2.0 * math.pi / LAGS)
        weight = np.where(freq == 0, 1.0, 2.0)[:, None] / math.sqrt(WINDOWS * LAGS)
        rows += [weight * np.cos(phase), -weight * np.sin(phase)]
    table = np.concatenate(rows, axis=0).astype(np.float32)
    high = table.astype(BF16)
    low = (table - high.astype(np.float32)).astype(BF16)
    return jnp.asarray(high), jnp.asarray(low)


def sums_for(x, core, source_spectra, receiver_spectra, bad_channels, place):
    far_low, far_high, up, down, own = source_pieces(source_spectra, place)

    def hop(piece, start, step):
        pair = (start % 4 * 2 + core, (start + step) % 4 * 2 + core)
        return lax.ppermute(piece, ("x", "core"), [pair])

    far_low, far_high = hop(far_low, x, 1), hop(far_high, x, -1)
    up, down = hop(up, x, 1), hop(down, x, -1)
    receiver_spectra, own = lax.optimization_barrier((receiver_spectra, own))
    blocks = receiver_blocks(receiver_spectra, place, bad_channels)
    rcv_at = lax.all_to_all(blocks, ("x", "y", "zl", "zh", "core"), 0, 0, tiled=True)
    far_low, far_high, _ = lax.optimization_barrier((far_low, far_high, blocks))
    far_low, far_high = hop(far_low, x + 1, 1), hop(far_high, x - 1, -1)
    pieces = (far_low, far_high, up, down, own)
    other = 1 - core
    shared = lax.ppermute(share(other, place, pieces), "core", [(core, other)])
    blocks = turn_source(core, place, pieces, shared)
    blocks, rcv_at = lax.optimization_barrier((blocks, rcv_at))
    src_at = lax.all_to_all(blocks, ("y", "zl", "zh", "core"), 0, 0, tiled=True)
    return cross_sums(place, src_at, rcv_at.reshape(32, 128, 128))


def on_device(source_spectra, receiver_spectra, source_block, bad_channels):
    x, zh, core = (lax.axis_index(a) for a in ("x", "zh", "core"))
    holder = source_block[0]
    place = jnp.stack(
        [x, (x * 4 + zh) * 2 + core, core, (x - holder // 8) % 4, (holder // 2) % 4]
    ).astype(jnp.int32)
    sums = lax.switch(
        holder // 8 * 2 + holder % 2,
        [functools.partial(sums_for, i // 2, i % 2) for i in range(8)],
        source_spectra,
        receiver_spectra,
        bad_channels,
        place,
    )
    mine = lax.all_to_all(sums, ("x", "zh", "core", "y", "zl"), 0, 0, tiled=True)
    high, low = inverse_table()
    return to_lags(mine, high, low).reshape(16, 16, LAGS)


def solution(mesh):
    fine = Mesh(mesh.devices.reshape(SIZES), AXES)
    win, rcv = AXES[:2], AXES[2:]
    return jax.shard_map(
        on_device,
        mesh=fine,
        in_specs=(P(win, rcv, None), P(win, rcv, None), P(), P()),
        out_specs=P(win, rcv, None),
        check_vma=False,
    )
```

```python
import functools
import math

import jax
import jax.numpy as jnp
import numpy as np
from jax import lax
from jax.experimental import pallas as pl
from jax.experimental.pallas import tpu as pltpu
from jax.sharding import Mesh
from jax.sharding import PartitionSpec as P

AXES = ("y", "zl", "x", "zh", "core")
SIZES = (4, 2, 4, 4, 2)
LAGS = 1024
HALF = 512
WINDOWS = 256
VMEM = 60 * 1024 * 1024
BF16 = jnp.bfloat16
F32 = jnp.float32


def whiten_parts(re, im, keep=None):
    power = re * re + im * im
    level = jnp.mean(power, axis=-1, keepdims=True)
    factor = lax.rsqrt(power + 0.1 * level + 1e-06)
    if keep is not None:
        factor = factor * keep
    return re * factor, im * factor


def source_kernel(place, src_ref, far_low, far_high, up, down, own, held):
    x = place[0]
    step, steps = pl.program_id(0), pl.num_programs(0)
    data = src_ref[...].astype(F32)
    re, im = (
        jnp.concatenate(
            [part[:, w * 16 + k * 8 : w * 16 + k * 8 + 8] for k in range(2) for w in range(8)],
            axis=1,
        )
        for part in whiten_parts(data[..., :HALF], data[..., HALF:])
    )
    for q in range(4):
        lanes = slice(q * 128, q * 128 + 128)
        held[q, :, :, :128] = re[..., lanes].astype(BF16)
        held[q, :, :, 128:] = im[..., lanes].astype(BF16)
    own[...] = held[x]
    up[...] = held[lax.rem(x + 1, 4)]
    down[...] = held[lax.rem(x + 3, 4)]

    @pl.when(step < steps // 2)
    def _():
        far_low[...] = held[lax.rem(x + 2, 4)]

    @pl.when(step >= steps // 2)
    def _():
        far_high[...] = held[lax.rem(x + 2, 4)]


def source_pieces(src, place):
    windows, sources, _ = src.shape
    block = 4
    steps = windows // block
    part = jax.ShapeDtypeStruct((windows // 2, sources, 256), BF16)
    piece = jax.ShapeDtypeStruct((windows, sources, 256), BF16)
    shape = (block, sources, 256)
    low = pl.BlockSpec(shape, lambda i, p: (jnp.minimum(i, steps // 2 - 1), 0, 0))
    high = pl.BlockSpec(shape, lambda i, p: (jnp.maximum(i - steps // 2, 0), 0, 0))
    plain = pl.BlockSpec(shape, lambda i, p: (i, 0, 0))
    return pl.pallas_call(
        source_kernel,
        out_shape=[part] * 2 + [piece] * 3,
        grid_spec=pltpu.PrefetchScalarGridSpec(
            num_scalar_prefetch=1,
            grid=(steps,),
            in_specs=[pl.BlockSpec((block, sources, LAGS), lambda i, p: (i, 0, 0))],
            out_specs=[low, high] + [plain] * 3,
            scratch_shapes=[pltpu.VMEM((4,) + shape, BF16)],
        ),
        compiler_params=pltpu.CompilerParams(vmem_limit_bytes=VMEM),
        cost_estimate=pl.CostEstimate(
            flops=40_000_000, bytes_accessed=16 * 2**20, transcendentals=2_000_000
        ),
    )(place, src)


def turn_pair(*parts):
    tall = jnp.concatenate(parts, axis=0).T
    low = lax.broadcasted_iota(jnp.int32, (64, 128), 1) < 64
    top, bottom = tall[:64], tall[64:]
    return (
        jnp.where(low, top, pltpu.roll(bottom, 64, axis=1)),
        jnp.where(low, pltpu.roll(top, 64, axis=1), bottom),
    )


def receiver_kernel(place, bad, rcv_ref, out_ref, held, turned):
    windows, chans, _ = rcv_ref.shape
    ids = place[1] * chans + lax.broadcasted_iota(jnp.int32, (chans, 128), 0)
    faulty = ids < 0
    for i in range(bad.shape[0]):
        faulty = faulty | (ids == bad[i])
    keep = jnp.where(faulty, 0.0, 1.0).astype(F32)[None, :, :1]
    group = 4

    @pl.loop(0, windows // group)
    def _(j):
        data = rcv_ref[pl.ds(j * group, group)].astype(F32)
        parts = whiten_parts(data[..., :HALF], data[..., HALF:], keep)
        rows = pl.ds(pl.multiple_of(j * group * chans, group * chans), group * chans)
        for q in range(4):
            for i in range(2):
                lanes = parts[i][..., q * 128 : q * 128 + 128]
                held[2 * q + i, rows, :] = lanes.reshape(group * chans, 128)

    @pl.loop(0, 4)
    def _(q):
        for c in range(0, chans, 2):
            pair = turn_pair(
                *(
                    held[2 * q + part, pl.ds(c + i, windows, stride=chans), :]
                    for i in range(2)
                    for part in range(2)
                )
            )
            for i in range(2):
                turned[pl.ds(q * 64 * chans + c + i, 64, stride=chans), :] = pair[i]

    @pl.loop(0, 8)
    def _(j):
        rows = turned[pl.ds(pl.multiple_of(j * 32 * chans, 32 * chans), 32 * chans), :]
        out_ref[pl.ds(j * 32, 32)] = rows.reshape(32, chans, 128).astype(BF16)


def receiver_blocks(rcv, place, bad):
    windows, chans, _ = rcv.shape
    return pl.pallas_call(
        receiver_kernel,
        out_shape=jax.ShapeDtypeStruct((256, chans, 128), BF16),
        grid_spec=pltpu.PrefetchScalarGridSpec(
            num_scalar_prefetch=2,
            grid=(1,),
            in_specs=[pl.BlockSpec(rcv.shape, lambda i, p, b: (0, 0, 0))],
            out_specs=pl.BlockSpec((256, chans, 128), lambda i, p, b: (0, 0, 0)),
            scratch_shapes=[
                pltpu.VMEM((8, windows * chans, 128), F32),
                pltpu.VMEM((256 * chans, 128), F32),
            ],
        ),
        compiler_params=pltpu.CompilerParams(vmem_limit_bytes=VMEM),
        cost_estimate=pl.CostEstimate(
            flops=20_000_000, bytes_accessed=2 * 2**20, transcendentals=300_000
        ),
    )(place, bad, rcv)


def take(away, pieces, core, target, sem):
    windows = target.shape[0]
    far_low, far_high, up, down, own = (ref.at[:, pl.ds(core * 64, 64)] for ref in pieces)

    def fetch(pairs):
        copies = [pltpu.make_async_copy(a, b, sem.at[i]) for i, (a, b) in enumerate(pairs)]
        for copy in copies:
            copy.start()
        for copy in copies:
            copy.wait()

    mid = windows // 2
    low, high = target.at[pl.ds(0, mid)], target.at[pl.ds(mid, mid)]
    for distance, pairs in (
        (0, [(own, target)]),
        (1, [(up, target)]),
        (2, [(far_low, low), (far_high, high)]),
        (3, [(down, target)]),
    ):
        pl.when(away == distance)(functools.partial(fetch, pairs))


def share_kernel(core, place, *refs):
    take(place[3], refs[:5], core, refs[5], refs[6])


def share(core, place, pieces):
    windows = pieces[-1].shape[0]
    return pl.pallas_call(
        functools.partial(share_kernel, core),
        out_shape=jax.ShapeDtypeStruct((windows, 64, 256), BF16),
        grid_spec=pltpu.PrefetchScalarGridSpec(
            num_scalar_prefetch=1,
            grid=(1,),
            in_specs=[pl.BlockSpec(memory_space=pl.ANY)] * 5,
            out_specs=pl.BlockSpec((windows, 64, 256), lambda i, p: (0, 0, 0)),
            scratch_shapes=[pltpu.SemaphoreType.DMA((2,))],
        ),
        compiler_params=pltpu.CompilerParams(vmem_limit_bytes=VMEM),
    )(place, *pieces)


def turn_kernel(holder_core, place, *refs):
    shared, out_ref, piece, held, turned, sem = refs[5:]
    windows = piece.shape[0]

    @pl.when(place[2] == holder_core)
    def _():
        take(place[3], refs[:5], holder_core, piece, sem)

    @pl.when(place[2] != holder_core)
    def _():
        copy = pltpu.make_async_copy(shared, piece, sem.at[0])
        copy.start()
        copy.wait()

    @pl.loop(0, windows // 4)
    def _(j):
        rows = pl.ds(pl.multiple_of(j * 256, 256), 256)
        for part in range(2):
            lanes = piece[pl.ds(j * 4, 4), :, part * 128 : part * 128 + 128]
            held[part, rows, :] = lanes.astype(F32).reshape(256, 128)

    @pl.loop(0, 8)
    def _(s):
        for w in range(0, 8, 2):
            pair = turn_pair(
                *(
                    held[part, pl.ds(w * 8 + i * 8 + s, windows, stride=64), :]
                    for i in range(2)
                    for part in range(2)
                )
            )
            for i in range(2):
                turned[pl.ds(s * 8 + w + i, 64, stride=64), :] = pair[i]

    @pl.loop(0, 8)
    def _(j):
        rows = turned[pl.ds(pl.multiple_of(j * 512, 512), 512), :]
        out_ref[pl.ds(j * 8, 8)] = rows.reshape(8, 64, 128).astype(BF16)


def turn_source(holder_core, place, pieces, shared):
    windows = pieces[-1].shape[0]
    return pl.pallas_call(
        functools.partial(turn_kernel, holder_core),
        out_shape=jax.ShapeDtypeStruct((64, 64, 128), BF16),
        grid_spec=pltpu.PrefetchScalarGridSpec(
            num_scalar_prefetch=1,
            grid=(1,),
            in_specs=[pl.BlockSpec(memory_space=pl.ANY)] * 6,
            out_specs=pl.BlockSpec((64, 64, 128), lambda i, p: (0, 0, 0)),
            scratch_shapes=[
                pltpu.VMEM((windows, 64, 256), BF16),
                pltpu.VMEM((2, windows * 64, 128), F32),
                pltpu.VMEM((64 * 64, 128), F32),
                pltpu.SemaphoreType.DMA((2,)),
            ],
        ),
        compiler_params=pltpu.CompilerParams(vmem_limit_bytes=VMEM),
    )(place, *pieces, shared)


def cross_kernel(place, src_ref, rcv_ref, out_ref, acc):
    row = lax.broadcasted_iota(jnp.int32, (512, 128), 0)
    col = lax.broadcasted_iota(jnp.int32, (512, 128), 1)
    spread = ((row // 8 == col % 64) & (row % 2 == col // 64)).astype(F32).astype(BF16)
    turned_row = (row // 2) % 2 == 1
    is_real = col % 64 < 32
    used = (row // 4) % 2 == col // 64
    zh = place[4]
    for win in range(8):
        base = (win * 4 + zh) * 2
        rows = jnp.concatenate([src_ref[base], src_ref[base + 1]], axis=0)
        plain = jnp.dot(spread, rows, preferred_element_type=F32)
        turned = jnp.where(
            is_real, -pltpu.roll(plain, 96, axis=1), pltpu.roll(plain, 32, axis=1)
        )
        left = jnp.where(used, jnp.where(turned_row, turned, plain), 0.0).astype(BF16)
        right = jnp.concatenate([rcv_ref[x * 8 + win] for x in range(4)], axis=0)
        part = lax.dot_general(left, right, (((1,), (1,)), ((), ())), preferred_element_type=F32)
        if win == 0:
            acc[...] = part
        else:
            acc[...] += part
    group = lax.broadcasted_iota(jnp.int32, (64, 128), 1) // 16
    for v in range(4):
        cols = slice(v * 128, v * 128 + 128)
        held = [acc[s * 64 : s * 64 + 64, cols] for s in range(8)]
        for bit in (4, 2, 1):
            low = (group & bit) == 0
            for s in range(8):
                if s & bit:
                    continue
                a, b = held[s], held[s + bit]
                held[s] = jnp.where(low, a, pltpu.roll(b, 16 * bit, axis=1))
                held[s + bit] = jnp.where(low, pltpu.roll(a, 128 - 16 * bit, axis=1), b)
        for g in range(8):
            first = (v * 8 + g) * 8
            out_ref[first : first + 8] = held[g].reshape(8, 8, 128).astype(BF16)


def cross_sums(place, src, rcv):
    return pl.pallas_call(
        cross_kernel,
        out_shape=jax.ShapeDtypeStruct((256, 8, 128), BF16),
        grid_spec=pltpu.PrefetchScalarGridSpec(
            num_scalar_prefetch=1,
            grid=(1,),
            in_specs=[
                pl.BlockSpec(src.shape, lambda i, p: (0, 0, 0)),
                pl.BlockSpec(rcv.shape, lambda i, p: (0, 0, 0)),
            ],
            out_specs=pl.BlockSpec((256, 8, 128), lambda i, p: (0, 0, 0)),
            scratch_shapes=[pltpu.VMEM((512, 512), F32)],
        ),
        compiler_params=pltpu.CompilerParams(vmem_limit_bytes=VMEM),
    )(place, src, rcv)


def lag_kernel(cross_ref, high_ref, low_ref, out_ref, wide, sorted_ref):
    @pl.when(pl.program_id(0) == 0)
    def _():
        wide[...] = cross_ref[...].astype(F32).reshape(2048, 128)
        for b in range(8):
            rows = wide[pl.ds(b, 256, stride=8), :].astype(BF16)
            sorted_ref[b // 2, :, b % 2 * 128 : b % 2 * 128 + 128] = rows

    total = None
    for b in range(4):
        for table in (high_ref, low_ref):
            part = lax.dot_general(
                sorted_ref[b],
                table[b * 256 : b * 256 + 256, :],
                (((0,), (0,)), ((), ())),
                preferred_element_type=F32,
            )
            total = part if total is None else total + part
    out_ref[...] = total


def to_lags(cross, high, low):
    return pl.pallas_call(
        lag_kernel,
        out_shape=jax.ShapeDtypeStruct((256, LAGS), F32),
        grid=(4,),
        in_specs=[
            pl.BlockSpec((256, 8, 128), lambda i: (0, 0, 0)),
            pl.BlockSpec((1024, 256), lambda i: (0, i)),
            pl.BlockSpec((1024, 256), lambda i: (0, i)),
        ],
        out_specs=pl.BlockSpec((256, 256), lambda i: (0, i)),
        scratch_shapes=[pltpu.VMEM((2048, 128), F32), pltpu.VMEM((4, 256, 256), BF16)],
        compiler_params=pltpu.CompilerParams(vmem_limit_bytes=VMEM),
    )(cross, high, low)


def inverse_table():
    x, zh, core, win = np.meshgrid(
        np.arange(4), np.arange(4), np.arange(2), np.arange(8), indexing="ij"
    )
    place = (x * 128 + (win * 4 + zh) * 2 + core).reshape(-1)
    lag = np.arange(LAGS)
    rows = []
    for j in range(2):
        freq = place + 64 * j
        phase = (freq[:, None] * lag[None, :] % LAGS) * (2.0 * math.pi / LAGS)
        weight = np.where(freq == 0, 1.0, 2.0)[:, None] / math.sqrt(WINDOWS * LAGS)
        rows += [weight * np.cos(phase), -weight * np.sin(phase)]
    table = np.concatenate(rows, axis=0).astype(np.float32)
    high = table.astype(BF16)
    low = (table - high.astype(np.float32)).astype(BF16)
    return jnp.asarray(high), jnp.asarray(low)


def exchange(x, core, pieces, receiver_spectra, bad_channels, place):
    far_low, far_high, up, down, own = pieces

    def hop(piece, start, step):
        pair = (start % 4 * 2 + core, (start + step) % 4 * 2 + core)
        return lax.ppermute(piece, ("x", "core"), [pair])

    far_low, far_high = hop(far_low, x, 1), hop(far_high, x, -1)
    up, down = hop(up, x, 1), hop(down, x, -1)
    blocks = receiver_blocks(receiver_spectra, place, bad_channels)
    rcv_at = lax.all_to_all(blocks, ("x", "y", "zl", "zh", "core"), 0, 0, tiled=True)
    far_low, far_high, _ = lax.optimization_barrier((far_low, far_high, blocks))
    far_low, far_high = hop(far_low, x + 1, 1), hop(far_high, x - 1, -1)
    pieces = (far_low, far_high, up, down, own)
    other = 1 - core
    shared = lax.ppermute(share(other, place, pieces), "core", [(core, other)])
    return turn_source(core, place, pieces, shared), rcv_at


def on_device(source_spectra, receiver_spectra, source_block, bad_channels):
    x, zh, core = (lax.axis_index(a) for a in ("x", "zh", "core"))
    holder = source_block[0]
    place = jnp.stack(
        [x, (x * 4 + zh) * 2 + core, core, (x - holder // 8) % 4, (holder // 2) % 4]
    ).astype(jnp.int32)
    src_blocks, rcv_at = lax.switch(
        holder // 8 * 2 + holder % 2,
        [functools.partial(exchange, i // 2, i % 2) for i in range(8)],
        tuple(source_pieces(source_spectra, place)),
        receiver_spectra,
        bad_channels,
        place,
    )
    src_at = lax.all_to_all(src_blocks, ("y", "zl", "zh", "core"), 0, 0, tiled=True)
    sums = cross_sums(place, src_at, rcv_at.reshape(32, 128, 128))
    mine = lax.all_to_all(sums, ("x", "zh", "core", "y", "zl"), 0, 0, tiled=True)
    high, low = inverse_table()
    return to_lags(mine, high, low).reshape(16, 16, LAGS)


def solution(mesh):
    fine = Mesh(mesh.devices.reshape(SIZES), AXES)
    win, rcv = AXES[:2], AXES[2:]
    return jax.shard_map(
        on_device,
        mesh=fine,
        in_specs=(P(win, rcv, None), P(win, rcv, None), P(), P()),
        out_specs=P(win, rcv, None),
        check_vma=False,
    )
```

```python
import functools
import math

import jax
import jax.numpy as jnp
import numpy as np
from jax import lax
from jax.experimental import pallas as pl
from jax.experimental.pallas import tpu as pltpu
from jax.sharding import Mesh
from jax.sharding import PartitionSpec as P

AXES = ("y", "zl", "x", "zh", "core")
SIZES = (4, 2, 4, 4, 2)
LAGS = 1024
HALF = 512
WINDOWS = 256
VMEM = 60 * 1024 * 1024
BF16 = jnp.bfloat16
F32 = jnp.float32


def whiten_parts(re, im, keep=None):
    power = re * re + im * im
    level = jnp.mean(power, axis=-1, keepdims=True)
    factor = lax.rsqrt(power + 0.1 * level + 1e-06)
    if keep is not None:
        factor = factor * keep
    return re * factor, im * factor


def source_kernel(place, src_ref, far_low, far_high, up, down, own, held):
    x = place[0]
    step, steps = pl.program_id(0), pl.num_programs(0)
    data = src_ref[...].astype(F32)
    re, im = (
        jnp.concatenate(
            [part[:, w * 16 + k * 8 : w * 16 + k * 8 + 8] for k in range(2) for w in range(8)],
            axis=1,
        )
        for part in whiten_parts(data[..., :HALF], data[..., HALF:])
    )
    for q in range(4):
        lanes = slice(q * 128, q * 128 + 128)
        held[q, :, :, :128] = re[..., lanes].astype(BF16)
        held[q, :, :, 128:] = im[..., lanes].astype(BF16)
    own[...] = held[x]
    up[...] = held[lax.rem(x + 1, 4)]
    down[...] = held[lax.rem(x + 3, 4)]

    @pl.when(step < steps // 2)
    def _():
        far_low[...] = held[lax.rem(x + 2, 4)]

    @pl.when(step >= steps // 2)
    def _():
        far_high[...] = held[lax.rem(x + 2, 4)]


def source_pieces(src, place):
    windows, sources, _ = src.shape
    block = 4
    steps = windows // block
    part = jax.ShapeDtypeStruct((windows // 2, sources, 256), BF16)
    piece = jax.ShapeDtypeStruct((windows, sources, 256), BF16)
    shape = (block, sources, 256)
    low = pl.BlockSpec(shape, lambda i, p: (jnp.minimum(i, steps // 2 - 1), 0, 0))
    high = pl.BlockSpec(shape, lambda i, p: (jnp.maximum(i - steps // 2, 0), 0, 0))
    plain = pl.BlockSpec(shape, lambda i, p: (i, 0, 0))
    return pl.pallas_call(
        source_kernel,
        out_shape=[part] * 2 + [piece] * 3,
        grid_spec=pltpu.PrefetchScalarGridSpec(
            num_scalar_prefetch=1,
            grid=(steps,),
            in_specs=[pl.BlockSpec((block, sources, LAGS), lambda i, p: (i, 0, 0))],
            out_specs=[low, high] + [plain] * 3,
            scratch_shapes=[pltpu.VMEM((4,) + shape, BF16)],
        ),
        compiler_params=pltpu.CompilerParams(vmem_limit_bytes=VMEM),
        cost_estimate=pl.CostEstimate(
            flops=40_000_000, bytes_accessed=16 * 2**20, transcendentals=2_000_000
        ),
    )(place, src)


def turn_pair(*parts):
    tall = jnp.concatenate(parts, axis=0).T
    low = lax.broadcasted_iota(jnp.int32, (64, 128), 1) < 64
    top, bottom = tall[:64], tall[64:]
    return (
        jnp.where(low, top, pltpu.roll(bottom, 64, axis=1)),
        jnp.where(low, pltpu.roll(top, 64, axis=1), bottom),
    )


def receiver_kernel(place, bad, rcv_ref, out_ref, held, turned):
    windows, chans, _ = rcv_ref.shape
    ids = place[1] * chans + lax.broadcasted_iota(jnp.int32, (chans, 128), 0)
    faulty = ids < 0
    for i in range(bad.shape[0]):
        faulty = faulty | (ids == bad[i])
    keep = jnp.where(faulty, 0.0, 1.0).astype(F32)[None, :, :1]
    group = 4

    @pl.loop(0, windows // group)
    def _(j):
        data = rcv_ref[pl.ds(j * group, group)].astype(F32)
        parts = whiten_parts(data[..., :HALF], data[..., HALF:], keep)
        rows = pl.ds(pl.multiple_of(j * group * chans, group * chans), group * chans)
        for q in range(4):
            for i in range(2):
                lanes = parts[i][..., q * 128 : q * 128 + 128]
                held[2 * q + i, rows, :] = lanes.reshape(group * chans, 128)

    @pl.loop(0, 4)
    def _(q):
        ahead = lax.rem(q + 4 - place[0], 4)
        for c in range(0, chans, 2):
            pair = turn_pair(
                *(
                    held[2 * q + part, pl.ds(c + i, windows, stride=chans), :]
                    for i in range(2)
                    for part in range(2)
                )
            )
            for i in range(2):
                turned[pl.ds(ahead * chans + c + i, 64, stride=4 * chans), :] = pair[i]

    @pl.loop(0, 8)
    def _(j):
        rows = turned[pl.ds(pl.multiple_of(j * 32 * chans, 32 * chans), 32 * chans), :]
        out_ref[pl.ds(j * 8, 8)] = rows.reshape(8, 4 * chans, 128).astype(BF16)


def receiver_blocks(rcv, place, bad):
    windows, chans, _ = rcv.shape
    return pl.pallas_call(
        receiver_kernel,
        out_shape=jax.ShapeDtypeStruct((64, 4 * chans, 128), BF16),
        grid_spec=pltpu.PrefetchScalarGridSpec(
            num_scalar_prefetch=2,
            grid=(1,),
            in_specs=[pl.BlockSpec(rcv.shape, lambda i, p, b: (0, 0, 0))],
            out_specs=pl.BlockSpec((64, 4 * chans, 128), lambda i, p, b: (0, 0, 0)),
            scratch_shapes=[
                pltpu.VMEM((8, windows * chans, 128), F32),
                pltpu.VMEM((256 * chans, 128), F32),
            ],
        ),
        compiler_params=pltpu.CompilerParams(vmem_limit_bytes=VMEM),
        cost_estimate=pl.CostEstimate(
            flops=20_000_000, bytes_accessed=2 * 2**20, transcendentals=300_000
        ),
    )(place, bad, rcv)


def take(away, pieces, core, target, sem):
    windows = target.shape[0]
    far_low, far_high, up, down, own = (ref.at[:, pl.ds(core * 64, 64)] for ref in pieces)

    def fetch(pairs):
        copies = [pltpu.make_async_copy(a, b, sem.at[i]) for i, (a, b) in enumerate(pairs)]
        for copy in copies:
            copy.start()
        for copy in copies:
            copy.wait()

    mid = windows // 2
    low, high = target.at[pl.ds(0, mid)], target.at[pl.ds(mid, mid)]
    for distance, pairs in (
        (0, [(own, target)]),
        (1, [(up, target)]),
        (2, [(far_low, low), (far_high, high)]),
        (3, [(down, target)]),
    ):
        pl.when(away == distance)(functools.partial(fetch, pairs))


def share_kernel(core, place, *refs):
    take(place[3], refs[:5], core, refs[5], refs[6])


def share(core, place, pieces):
    windows = pieces[-1].shape[0]
    return pl.pallas_call(
        functools.partial(share_kernel, core),
        out_shape=jax.ShapeDtypeStruct((windows, 64, 256), BF16),
        grid_spec=pltpu.PrefetchScalarGridSpec(
            num_scalar_prefetch=1,
            grid=(1,),
            in_specs=[pl.BlockSpec(memory_space=pl.ANY)] * 5,
            out_specs=pl.BlockSpec((windows, 64, 256), lambda i, p: (0, 0, 0)),
            scratch_shapes=[pltpu.SemaphoreType.DMA((2,))],
        ),
        compiler_params=pltpu.CompilerParams(vmem_limit_bytes=VMEM),
    )(place, *pieces)


def turn_kernel(holder_core, place, *refs):
    shared, out_ref, piece, held, turned, sem = refs[5:]
    windows = piece.shape[0]

    @pl.when(place[2] == holder_core)
    def _():
        take(place[3], refs[:5], holder_core, piece, sem)

    @pl.when(place[2] != holder_core)
    def _():
        copy = pltpu.make_async_copy(shared, piece, sem.at[0])
        copy.start()
        copy.wait()

    @pl.loop(0, windows // 4)
    def _(j):
        rows = pl.ds(pl.multiple_of(j * 256, 256), 256)
        for part in range(2):
            lanes = piece[pl.ds(j * 4, 4), :, part * 128 : part * 128 + 128]
            held[part, rows, :] = lanes.astype(F32).reshape(256, 128)

    @pl.loop(0, 8)
    def _(s):
        for w in range(0, 8, 2):
            pair = turn_pair(
                *(
                    held[part, pl.ds(w * 8 + i * 8 + s, windows, stride=64), :]
                    for i in range(2)
                    for part in range(2)
                )
            )
            for i in range(2):
                turned[pl.ds(s * 8 + w + i, 64, stride=64), :] = pair[i]

    @pl.loop(0, 8)
    def _(j):
        rows = turned[pl.ds(pl.multiple_of(j * 512, 512), 512), :]
        out_ref[pl.ds(j * 8, 8)] = rows.reshape(8, 64, 128).astype(BF16)


def turn_source(holder_core, place, pieces, shared):
    windows = pieces[-1].shape[0]
    return pl.pallas_call(
        functools.partial(turn_kernel, holder_core),
        out_shape=jax.ShapeDtypeStruct((64, 64, 128), BF16),
        grid_spec=pltpu.PrefetchScalarGridSpec(
            num_scalar_prefetch=1,
            grid=(1,),
            in_specs=[pl.BlockSpec(memory_space=pl.ANY)] * 6,
            out_specs=pl.BlockSpec((64, 64, 128), lambda i, p: (0, 0, 0)),
            scratch_shapes=[
                pltpu.VMEM((windows, 64, 256), BF16),
                pltpu.VMEM((2, windows * 64, 128), F32),
                pltpu.VMEM((64 * 64, 128), F32),
                pltpu.SemaphoreType.DMA((2,)),
            ],
        ),
        compiler_params=pltpu.CompilerParams(vmem_limit_bytes=VMEM),
    )(place, *pieces, shared)


def cross_kernel(place, src_ref, *refs):
    rcv_refs, out_ref, left = refs[:4], refs[4], refs[5]
    row = lax.broadcasted_iota(jnp.int32, (512, 256), 0)
    col = lax.broadcasted_iota(jnp.int32, (512, 256), 1)
    wanted = ((row // 2) % 2) * 128 + (row % 2) * 64 + row // 8
    spread = (wanted == col).astype(F32).astype(BF16)
    lane = lax.broadcasted_iota(jnp.int32, (512, 128), 1)
    used = (lax.broadcasted_iota(jnp.int32, (512, 128), 0) // 4) % 2 == lane // 64
    is_real = lane[:128] % 64 < 32
    zh = place[4]
    for win in range(8):
        base = (win * 4 + zh) * 2
        plain = jnp.concatenate([src_ref[base], src_ref[base + 1]], axis=0)
        wide = plain.astype(F32)
        turned = jnp.where(is_real, -pltpu.roll(wide, 96, axis=1), pltpu.roll(wide, 32, axis=1))
        both = jnp.concatenate([plain, turned.astype(BF16)], axis=0)
        rows = jnp.dot(spread, both, preferred_element_type=F32)
        left[:, win * 128 : win * 128 + 128] = jnp.where(used, rows, 0.0).astype(BF16)
    group = lax.broadcasted_iota(jnp.int32, (64, 128), 1) // 16
    for ahead in range(4):
        right = jnp.concatenate(
            [rcv_refs[ahead][w * 8 : w * 8 + 8].reshape(128, 128) for w in range(8)], axis=1
        )
        sums = lax.dot_general(
            left[...], right, (((1,), (1,)), ((), ())), preferred_element_type=F32
        )
        held = [sums[s * 64 : s * 64 + 64] for s in range(8)]
        for bit in (4, 2, 1):
            low = (group & bit) == 0
            for s in range(8):
                if s & bit:
                    continue
                a, b = held[s], held[s + bit]
                held[s] = jnp.where(low, a, pltpu.roll(b, 16 * bit, axis=1))
                held[s + bit] = jnp.where(low, pltpu.roll(a, 128 - 16 * bit, axis=1), b)
        first = lax.rem(place[0] + 4 - ahead, 4) * 64
        for g in range(8):
            out_ref[pl.ds(first + g * 8, 8)] = held[g].reshape(8, 8, 128).astype(BF16)


def cross_sums(place, src, rcvs):
    return pl.pallas_call(
        cross_kernel,
        out_shape=jax.ShapeDtypeStruct((256, 8, 128), BF16),
        grid_spec=pltpu.PrefetchScalarGridSpec(
            num_scalar_prefetch=1,
            grid=(1,),
            in_specs=[pl.BlockSpec(a.shape, lambda i, p: (0, 0, 0)) for a in (src, *rcvs)],
            out_specs=pl.BlockSpec((256, 8, 128), lambda i, p: (0, 0, 0)),
            scratch_shapes=[pltpu.VMEM((512, 1024), BF16)],
        ),
        compiler_params=pltpu.CompilerParams(vmem_limit_bytes=VMEM),
    )(place, src, *rcvs)


def lag_kernel(cross_ref, high_ref, low_ref, out_ref, wide, sums):
    @pl.when(pl.program_id(0) == 0)
    def _():
        wide[...] = cross_ref[...].astype(F32).reshape(2048, 128)
        for b in range(8):
            rows, cols = b % 2 * 128, b // 2 * 256
            sums[rows : rows + 128, cols : cols + 256] = (
                wide[pl.ds(b, 256, stride=8), :].T.astype(BF16)
            )

    out_ref[...] = jnp.dot(sums[...], high_ref[...], preferred_element_type=F32) + jnp.dot(
        sums[...], low_ref[...], preferred_element_type=F32
    )


def to_lags(cross, high, low):
    return pl.pallas_call(
        lag_kernel,
        out_shape=jax.ShapeDtypeStruct((256, LAGS), F32),
        grid=(4,),
        in_specs=[
            pl.BlockSpec((256, 8, 128), lambda i: (0, 0, 0)),
            pl.BlockSpec((1024, 256), lambda i: (0, i)),
            pl.BlockSpec((1024, 256), lambda i: (0, i)),
        ],
        out_specs=pl.BlockSpec((256, 256), lambda i: (0, i)),
        scratch_shapes=[pltpu.VMEM((2048, 128), F32), pltpu.VMEM((256, 1024), BF16)],
        compiler_params=pltpu.CompilerParams(vmem_limit_bytes=VMEM),
    )(cross, high, low)


def inverse_table():
    x, zh, core, win = np.meshgrid(
        np.arange(4), np.arange(4), np.arange(2), np.arange(8), indexing="ij"
    )
    place = (x * 128 + (win * 4 + zh) * 2 + core).reshape(-1)
    lag = np.arange(LAGS)
    rows = []
    for j in range(2):
        freq = place + 64 * j
        phase = (freq[:, None] * lag[None, :] % LAGS) * (2.0 * math.pi / LAGS)
        weight = np.where(freq == 0, 1.0, 2.0)[:, None] / math.sqrt(WINDOWS * LAGS)
        rows += [weight * np.cos(phase), -weight * np.sin(phase)]
    table = np.concatenate(rows, axis=0).astype(np.float32)
    high = table.astype(BF16)
    low = (table - high.astype(np.float32)).astype(BF16)
    return jnp.asarray(high), jnp.asarray(low)


def exchange(x, core, pieces, receiver_spectra, bad_channels, place):
    far_low, far_high, up, down, own = pieces

    def hop(piece, start, step):
        pair = (start % 4 * 2 + core, (start + step) % 4 * 2 + core)
        return lax.ppermute(piece, ("x", "core"), [pair])

    far_low, far_high = hop(far_low, x, 1), hop(far_high, x, -1)
    up, down = hop(up, x, 1), hop(down, x, -1)
    blocks = receiver_blocks(receiver_spectra, place, bad_channels)
    rcv_at = lax.all_to_all(blocks, ("y", "zl", "zh", "core"), 0, 0, tiled=True)
    far_low, far_high, _ = lax.optimization_barrier((far_low, far_high, blocks))
    far_low, far_high = hop(far_low, x + 1, 1), hop(far_high, x - 1, -1)
    pieces = (far_low, far_high, up, down, own)
    other = 1 - core
    shared = lax.ppermute(share(other, place, pieces), "core", [(core, other)])
    return turn_source(core, place, pieces, shared), rcv_at


def on_device(source_spectra, receiver_spectra, source_block, bad_channels):
    x, zh, core = (lax.axis_index(a) for a in ("x", "zh", "core"))
    holder = source_block[0]
    place = jnp.stack(
        [x, (x * 4 + zh) * 2 + core, core, (x - holder // 8) % 4, (holder // 2) % 4]
    ).astype(jnp.int32)
    src_blocks, rcv_at = lax.switch(
        holder // 8 * 2 + holder % 2,
        [functools.partial(exchange, i // 2, i % 2) for i in range(8)],
        tuple(source_pieces(source_spectra, place)),
        receiver_spectra,
        bad_channels,
        place,
    )
    chans = rcv_at.shape[1] // 4
    rcvs = [rcv_at[:, i * chans : i * chans + chans] for i in range(4)]
    for i in (2, 1, 3):
        rcvs[i] = lax.ppermute(rcvs[i], "x", [(j, (j + i) % 4) for j in range(4)])
    src_at = lax.all_to_all(src_blocks, ("y", "zl", "zh", "core"), 0, 0, tiled=True)
    sums = cross_sums(place, src_at, rcvs)
    mine = lax.all_to_all(sums, ("x", "zh", "core", "y", "zl"), 0, 0, tiled=True)
    high, low = inverse_table()
    return to_lags(mine, high, low).reshape(16, 16, LAGS)


def solution(mesh):
    fine = Mesh(mesh.devices.reshape(SIZES), AXES)
    win, rcv = AXES[:2], AXES[2:]
    return jax.shard_map(
        on_device,
        mesh=fine,
        in_specs=(P(win, rcv, None), P(win, rcv, None), P(), P()),
        out_specs=P(win, rcv, None),
        check_vma=False,
    )
```

```python
import functools
import math

import jax
import jax.numpy as jnp
import numpy as np
from jax import lax
from jax.experimental import pallas as pl
from jax.experimental.pallas import tpu as pltpu
from jax.sharding import Mesh
from jax.sharding import PartitionSpec as P

AXES = ("y", "zl", "x", "zh", "core")
SIZES = (4, 2, 4, 4, 2)
LAGS = 1024
HALF = 512
WINDOWS = 256
VMEM = 60 * 1024 * 1024
BF16 = jnp.bfloat16
F32 = jnp.float32


def whiten_parts(re, im, keep=None):
    power = re * re + im * im
    level = jnp.mean(power, axis=-1, keepdims=True)
    factor = lax.rsqrt(power + 0.1 * level + 1e-06)
    if keep is not None:
        factor = factor * keep
    return re * factor, im * factor


def source_kernel(place, src_ref, far_low, far_high, up, down, own):
    step, steps = pl.program_id(0), pl.num_programs(0)

    def part(start):
        return src_ref[:, :, pl.ds(start, 128)].astype(F32)

    total = None
    for q in range(4):
        re, im = part(q * 128), part(HALF + q * 128)
        power = re * re + im * im
        total = power if total is None else total + power
    level = 0.1 * (jnp.sum(total, axis=-1, keepdims=True) / HALF) + 1e-06

    def emit(ahead, out):
        start = lax.rem(place[0] + ahead, 4) * 128
        re = part(pl.multiple_of(start, 128))
        im = part(pl.multiple_of(HALF + start, 128))
        factor = lax.rsqrt(re * re + im * im + level)
        for i, value in enumerate((re * factor, im * factor)):
            rows = [
                value[:, w * 16 + k * 8 : w * 16 + k * 8 + 8] for k in range(2) for w in range(8)
            ]
            out[:, :, i * 128 : i * 128 + 128] = jnp.concatenate(rows, axis=1).astype(BF16)

    emit(0, own)
    emit(1, up)
    emit(3, down)
    pl.when(step < steps // 2)(functools.partial(emit, 2, far_low))
    pl.when(step >= steps // 2)(functools.partial(emit, 2, far_high))


def source_pieces(src, place):
    windows, sources, _ = src.shape
    block = 8
    steps = windows // block
    part = jax.ShapeDtypeStruct((windows // 2, sources, 256), BF16)
    piece = jax.ShapeDtypeStruct((windows, sources, 256), BF16)
    shape = (block, sources, 256)
    low = pl.BlockSpec(shape, lambda i, p: (jnp.minimum(i, steps // 2 - 1), 0, 0))
    high = pl.BlockSpec(shape, lambda i, p: (jnp.maximum(i - steps // 2, 0), 0, 0))
    plain = pl.BlockSpec(shape, lambda i, p: (i, 0, 0))
    return pl.pallas_call(
        source_kernel,
        out_shape=[part] * 2 + [piece] * 3,
        grid_spec=pltpu.PrefetchScalarGridSpec(
            num_scalar_prefetch=1,
            grid=(steps,),
            in_specs=[pl.BlockSpec((block, sources, LAGS), lambda i, p: (i, 0, 0))],
            out_specs=[low, high] + [plain] * 3,
        ),
        compiler_params=pltpu.CompilerParams(vmem_limit_bytes=VMEM),
        cost_estimate=pl.CostEstimate(
            flops=40_000_000, bytes_accessed=16 * 2**20, transcendentals=2_000_000
        ),
    )(place, src)


def turn_pair(*parts):
    tall = jnp.concatenate(parts, axis=0).T
    low = lax.broadcasted_iota(jnp.int32, (64, 128), 1) < 64
    top, bottom = tall[:64], tall[64:]
    return (
        jnp.where(low, top, pltpu.roll(bottom, 64, axis=1)),
        jnp.where(low, pltpu.roll(top, 64, axis=1), bottom),
    )


def receiver_kernel(place, bad, rcv_ref, out_ref, held, turned):
    windows, chans, _ = rcv_ref.shape
    ids = place[1] * chans + lax.broadcasted_iota(jnp.int32, (chans, 128), 0)
    faulty = ids < 0
    for i in range(bad.shape[0]):
        faulty = faulty | (ids == bad[i])
    keep = jnp.where(faulty, 0.0, 1.0).astype(F32)[None, :, :1]
    group = 4

    @pl.loop(0, windows // group)
    def _(j):
        data = rcv_ref[pl.ds(j * group, group)].astype(F32)
        parts = whiten_parts(data[..., :HALF], data[..., HALF:], keep)
        rows = pl.ds(pl.multiple_of(j * group * chans, group * chans), group * chans)
        for q in range(4):
            for i in range(2):
                lanes = parts[i][..., q * 128 : q * 128 + 128]
                held[2 * q + i, rows, :] = lanes.reshape(group * chans, 128)

    @pl.loop(0, 4)
    def _(q):
        for c in range(0, chans, 2):
            pair = turn_pair(
                *(
                    held[2 * q + part, pl.ds(c + i, windows, stride=chans), :]
                    for i in range(2)
                    for part in range(2)
                )
            )
            for i in range(2):
                turned[pl.ds(q * 64 * chans + c + i, 64, stride=chans), :] = pair[i]

    @pl.loop(0, 8)
    def _(j):
        rows = turned[pl.ds(pl.multiple_of(j * 32 * chans, 32 * chans), 32 * chans), :]
        out_ref[pl.ds(j * 32, 32)] = rows.reshape(32, chans, 128).astype(BF16)


def receiver_blocks(rcv, place, bad):
    windows, chans, _ = rcv.shape
    return pl.pallas_call(
        receiver_kernel,
        out_shape=jax.ShapeDtypeStruct((256, chans, 128), BF16),
        grid_spec=pltpu.PrefetchScalarGridSpec(
            num_scalar_prefetch=2,
            grid=(1,),
            in_specs=[pl.BlockSpec(rcv.shape, lambda i, p, b: (0, 0, 0))],
            out_specs=pl.BlockSpec((256, chans, 128), lambda i, p, b: (0, 0, 0)),
            scratch_shapes=[
                pltpu.VMEM((8, windows * chans, 128), F32),
                pltpu.VMEM((256 * chans, 128), F32),
            ],
        ),
        compiler_params=pltpu.CompilerParams(vmem_limit_bytes=VMEM),
        cost_estimate=pl.CostEstimate(
            flops=20_000_000, bytes_accessed=2 * 2**20, transcendentals=300_000
        ),
    )(place, bad, rcv)


def take(away, pieces, core, target, sem):
    windows = target.shape[0]
    far_low, far_high, up, down, own = (ref.at[:, pl.ds(core * 64, 64)] for ref in pieces)

    def fetch(pairs):
        copies = [pltpu.make_async_copy(a, b, sem.at[i]) for i, (a, b) in enumerate(pairs)]
        for copy in copies:
            copy.start()
        for copy in copies:
            copy.wait()

    mid = windows // 2
    low, high = target.at[pl.ds(0, mid)], target.at[pl.ds(mid, mid)]
    for distance, pairs in (
        (0, [(own, target)]),
        (1, [(up, target)]),
        (2, [(far_low, low), (far_high, high)]),
        (3, [(down, target)]),
    ):
        pl.when(away == distance)(functools.partial(fetch, pairs))


def share_kernel(core, place, *refs):
    take(place[3], refs[:5], core, refs[5], refs[6])


def share(core, place, pieces):
    windows = pieces[-1].shape[0]
    return pl.pallas_call(
        functools.partial(share_kernel, core),
        out_shape=jax.ShapeDtypeStruct((windows, 64, 256), BF16),
        grid_spec=pltpu.PrefetchScalarGridSpec(
            num_scalar_prefetch=1,
            grid=(1,),
            in_specs=[pl.BlockSpec(memory_space=pl.ANY)] * 5,
            out_specs=pl.BlockSpec((windows, 64, 256), lambda i, p: (0, 0, 0)),
            scratch_shapes=[pltpu.SemaphoreType.DMA((2,))],
        ),
        compiler_params=pltpu.CompilerParams(vmem_limit_bytes=VMEM),
    )(place, *pieces)


def turn_kernel(holder_core, place, *refs):
    shared, out_ref, piece, held, turned, sem = refs[5:]
    windows = piece.shape[0]

    @pl.when(place[2] == holder_core)
    def _():
        take(place[3], refs[:5], holder_core, piece, sem)

    @pl.when(place[2] != holder_core)
    def _():
        copy = pltpu.make_async_copy(shared, piece, sem.at[0])
        copy.start()
        copy.wait()

    @pl.loop(0, windows // 4)
    def _(j):
        rows = pl.ds(pl.multiple_of(j * 256, 256), 256)
        for part in range(2):
            lanes = piece[pl.ds(j * 4, 4), :, part * 128 : part * 128 + 128]
            held[part, rows, :] = lanes.astype(F32).reshape(256, 128)

    @pl.loop(0, 8)
    def _(s):
        for w in range(0, 8, 2):
            pair = turn_pair(
                *(
                    held[part, pl.ds(w * 8 + i * 8 + s, windows, stride=64), :]
                    for i in range(2)
                    for part in range(2)
                )
            )
            for i in range(2):
                turned[pl.ds(s * 8 + w + i, 64, stride=64), :] = pair[i]

    @pl.loop(0, 8)
    def _(j):
        rows = turned[pl.ds(pl.multiple_of(j * 512, 512), 512), :]
        out_ref[pl.ds(j * 8, 8)] = rows.reshape(8, 64, 128).astype(BF16)


def turn_source(holder_core, place, pieces, shared):
    windows = pieces[-1].shape[0]
    return pl.pallas_call(
        functools.partial(turn_kernel, holder_core),
        out_shape=jax.ShapeDtypeStruct((64, 64, 128), BF16),
        grid_spec=pltpu.PrefetchScalarGridSpec(
            num_scalar_prefetch=1,
            grid=(1,),
            in_specs=[pl.BlockSpec(memory_space=pl.ANY)] * 6,
            out_specs=pl.BlockSpec((64, 64, 128), lambda i, p: (0, 0, 0)),
            scratch_shapes=[
                pltpu.VMEM((windows, 64, 256), BF16),
                pltpu.VMEM((2, windows * 64, 128), F32),
                pltpu.VMEM((64 * 64, 128), F32),
                pltpu.SemaphoreType.DMA((2,)),
            ],
        ),
        compiler_params=pltpu.CompilerParams(vmem_limit_bytes=VMEM),
    )(place, *pieces, shared)


def cross_kernel(place, src_ref, rcv_ref, out_ref, left):
    row = lax.broadcasted_iota(jnp.int32, (512, 256), 0)
    col = lax.broadcasted_iota(jnp.int32, (512, 256), 1)
    wanted = ((row // 2) % 2) * 128 + (row % 2) * 64 + row // 8
    spread = (wanted == col).astype(F32).astype(BF16)
    lane = lax.broadcasted_iota(jnp.int32, (512, 128), 1)
    used = (lax.broadcasted_iota(jnp.int32, (512, 128), 0) // 4) % 2 == lane // 64
    is_real = lane[:128] % 64 < 32
    zh = place[4]
    for win in range(8):
        base = (win * 4 + zh) * 2
        plain = jnp.concatenate([src_ref[base], src_ref[base + 1]], axis=0)
        wide = plain.astype(F32)
        turned = jnp.where(is_real, -pltpu.roll(wide, 96, axis=1), pltpu.roll(wide, 32, axis=1))
        both = jnp.concatenate([plain, turned.astype(BF16)], axis=0)
        rows = jnp.dot(spread, both, preferred_element_type=F32)
        left[:, win * 128 : win * 128 + 128] = jnp.where(used, rows, 0.0).astype(BF16)
    group = lax.broadcasted_iota(jnp.int32, (64, 128), 1) // 16
    for x in range(4):
        right = jnp.concatenate([rcv_ref[x * 8 + win] for win in range(8)], axis=1)
        sums = lax.dot_general(
            left[...], right, (((1,), (1,)), ((), ())), preferred_element_type=F32
        )
        held = [sums[s * 64 : s * 64 + 64] for s in range(8)]
        for bit in (4, 2, 1):
            low = (group & bit) == 0
            for s in range(8):
                if s & bit:
                    continue
                a, b = held[s], held[s + bit]
                held[s] = jnp.where(low, a, pltpu.roll(b, 16 * bit, axis=1))
                held[s + bit] = jnp.where(low, pltpu.roll(a, 128 - 16 * bit, axis=1), b)
        for g in range(8):
            first = x * 64 + g * 8
            out_ref[first : first + 8] = held[g].reshape(8, 8, 128).astype(BF16)


def cross_sums(place, src, rcv):
    return pl.pallas_call(
        cross_kernel,
        out_shape=jax.ShapeDtypeStruct((256, 8, 128), BF16),
        grid_spec=pltpu.PrefetchScalarGridSpec(
            num_scalar_prefetch=1,
            grid=(1,),
            in_specs=[pl.BlockSpec(a.shape, lambda i, p: (0, 0, 0)) for a in (src, rcv)],
            out_specs=pl.BlockSpec((256, 8, 128), lambda i, p: (0, 0, 0)),
            scratch_shapes=[pltpu.VMEM((512, 1024), BF16)],
        ),
        compiler_params=pltpu.CompilerParams(vmem_limit_bytes=VMEM),
    )(place, src, rcv)


def lag_kernel(cross_ref, high_ref, low_ref, out_ref, wide, sums):
    @pl.when(pl.program_id(0) == 0)
    def _():
        wide[...] = cross_ref[...].astype(F32).reshape(2048, 128)
        for b in range(8):
            rows, cols = b % 2 * 128, b // 2 * 256
            sums[rows : rows + 128, cols : cols + 256] = (
                wide[pl.ds(b, 256, stride=8), :].T.astype(BF16)
            )

    out_ref[...] = jnp.dot(sums[...], high_ref[...], preferred_element_type=F32) + jnp.dot(
        sums[...], low_ref[...], preferred_element_type=F32
    )


def to_lags(cross, high, low):
    return pl.pallas_call(
        lag_kernel,
        out_shape=jax.ShapeDtypeStruct((256, LAGS), F32),
        grid=(2,),
        in_specs=[
            pl.BlockSpec((256, 8, 128), lambda i: (0, 0, 0)),
            pl.BlockSpec((1024, 512), lambda i: (0, i)),
            pl.BlockSpec((1024, 512), lambda i: (0, i)),
        ],
        out_specs=pl.BlockSpec((256, 512), lambda i: (0, i)),
        scratch_shapes=[pltpu.VMEM((2048, 128), F32), pltpu.VMEM((256, 1024), BF16)],
        compiler_params=pltpu.CompilerParams(vmem_limit_bytes=VMEM),
    )(cross, high, low)


def inverse_table():
    x, zh, core, win = np.meshgrid(
        np.arange(4), np.arange(4), np.arange(2), np.arange(8), indexing="ij"
    )
    place = (x * 128 + (win * 4 + zh) * 2 + core).reshape(-1)
    lag = np.arange(LAGS)
    rows = []
    for j in range(2):
        freq = place + 64 * j
        phase = (freq[:, None] * lag[None, :] % LAGS) * (2.0 * math.pi / LAGS)
        weight = np.where(freq == 0, 1.0, 2.0)[:, None] / math.sqrt(WINDOWS * LAGS)
        rows += [weight * np.cos(phase), -weight * np.sin(phase)]
    table = np.concatenate(rows, axis=0).astype(np.float32)
    high = table.astype(BF16)
    low = (table - high.astype(np.float32)).astype(BF16)
    return jnp.asarray(high), jnp.asarray(low)


def exchange(x, core, pieces, receiver_spectra, bad_channels, place):
    far_low, far_high, up, down, own = pieces

    def hop(piece, start, step):
        pair = (start % 4 * 2 + core, (start + step) % 4 * 2 + core)
        return lax.ppermute(piece, ("x", "core"), [pair])

    far_low, far_high = hop(far_low, x, 1), hop(far_high, x, -1)
    up, down = hop(up, x, 1), hop(down, x, -1)
    blocks = receiver_blocks(receiver_spectra, place, bad_channels)
    rcv_at = lax.all_to_all(blocks, ("x", "y", "zl", "zh", "core"), 0, 0, tiled=True)
    far_low, far_high, _ = lax.optimization_barrier((far_low, far_high, blocks))
    far_low, far_high = hop(far_low, x + 1, 1), hop(far_high, x - 1, -1)
    pieces = (far_low, far_high, up, down, own)
    other = 1 - core
    shared = lax.ppermute(share(other, place, pieces), "core", [(core, other)])
    return turn_source(core, place, pieces, shared), rcv_at


def on_device(source_spectra, receiver_spectra, source_block, bad_channels):
    x, zh, core = (lax.axis_index(a) for a in ("x", "zh", "core"))
    holder = source_block[0]
    place = jnp.stack(
        [x, (x * 4 + zh) * 2 + core, core, (x - holder // 8) % 4, (holder // 2) % 4]
    ).astype(jnp.int32)
    src_blocks, rcv_at = lax.switch(
        holder // 8 * 2 + holder % 2,
        [functools.partial(exchange, i // 2, i % 2) for i in range(8)],
        tuple(source_pieces(source_spectra, place)),
        receiver_spectra,
        bad_channels,
        place,
    )
    src_at = lax.all_to_all(src_blocks, ("y", "zl", "zh", "core"), 0, 0, tiled=True)
    sums = cross_sums(place, src_at, rcv_at.reshape(32, 128, 128))
    mine = lax.all_to_all(sums, ("x", "zh", "core", "y", "zl"), 0, 0, tiled=True)
    high, low = inverse_table()
    return to_lags(mine, high, low).reshape(16, 16, LAGS)


def solution(mesh):
    fine = Mesh(mesh.devices.reshape(SIZES), AXES)
    win, rcv = AXES[:2], AXES[2:]
    return jax.shard_map(
        on_device,
        mesh=fine,
        in_specs=(P(win, rcv, None), P(win, rcv, None), P(), P()),
        out_specs=P(win, rcv, None),
        check_vma=False,
    )
```

```python
import functools
import math

import jax
import jax.numpy as jnp
import numpy as np
from jax import lax
from jax.experimental import pallas as pl
from jax.experimental.pallas import tpu as pltpu
from jax.sharding import Mesh
from jax.sharding import PartitionSpec as P

AXES = ("y", "zl", "x", "zh", "core")
SIZES = (4, 2, 4, 4, 2)
LAGS = 1024
HALF = 512
WINDOWS = 256
VMEM = 60 * 1024 * 1024
BF16 = jnp.bfloat16
F32 = jnp.float32


def whiten_parts(re, im, keep=None):
    power = re * re + im * im
    level = jnp.mean(power, axis=-1, keepdims=True)
    factor = lax.rsqrt(power + 0.1 * level + 1e-06)
    if keep is not None:
        factor = factor * keep
    return re * factor, im * factor


def source_kernel(place, src_ref, far_low, far_high, up, down, own):
    step, steps = pl.program_id(0), pl.num_programs(0)

    def part(start):
        return src_ref[:, :, pl.ds(start, 128)].astype(F32)

    total = None
    for q in range(4):
        re, im = part(q * 128), part(HALF + q * 128)
        power = re * re + im * im
        total = power if total is None else total + power
    level = 0.1 * (jnp.sum(total, axis=-1, keepdims=True) / HALF) + 1e-06

    def emit(ahead, out):
        start = lax.rem(place[0] + ahead, 4) * 128
        re = part(pl.multiple_of(start, 128))
        im = part(pl.multiple_of(HALF + start, 128))
        factor = lax.rsqrt(re * re + im * im + level)
        for i, value in enumerate((re * factor, im * factor)):
            rows = [
                value[:, w * 16 + k * 8 : w * 16 + k * 8 + 8] for k in range(2) for w in range(8)
            ]
            out[:, :, i * 128 : i * 128 + 128] = jnp.concatenate(rows, axis=1).astype(BF16)

    emit(0, own)
    emit(1, up)
    emit(3, down)
    pl.when(step < steps // 2)(functools.partial(emit, 2, far_low))
    pl.when(step >= steps // 2)(functools.partial(emit, 2, far_high))


def source_pieces(src, place):
    windows, sources, _ = src.shape
    block = 8
    steps = windows // block
    part = jax.ShapeDtypeStruct((windows // 2, sources, 256), BF16)
    piece = jax.ShapeDtypeStruct((windows, sources, 256), BF16)
    shape = (block, sources, 256)
    low = pl.BlockSpec(shape, lambda i, p: (jnp.minimum(i, steps // 2 - 1), 0, 0))
    high = pl.BlockSpec(shape, lambda i, p: (jnp.maximum(i - steps // 2, 0), 0, 0))
    plain = pl.BlockSpec(shape, lambda i, p: (i, 0, 0))
    return pl.pallas_call(
        source_kernel,
        out_shape=[part] * 2 + [piece] * 3,
        grid_spec=pltpu.PrefetchScalarGridSpec(
            num_scalar_prefetch=1,
            grid=(steps,),
            in_specs=[pl.BlockSpec((block, sources, LAGS), lambda i, p: (i, 0, 0))],
            out_specs=[low, high] + [plain] * 3,
        ),
        compiler_params=pltpu.CompilerParams(vmem_limit_bytes=VMEM),
        cost_estimate=pl.CostEstimate(
            flops=40_000_000, bytes_accessed=16 * 2**20, transcendentals=2_000_000
        ),
    )(place, src)


def turn_pair(*parts):
    tall = jnp.concatenate(parts, axis=0).T
    low = lax.broadcasted_iota(jnp.int32, (64, 128), 1) < 64
    top, bottom = tall[:64], tall[64:]
    return (
        jnp.where(low, top, pltpu.roll(bottom, 64, axis=1)),
        jnp.where(low, pltpu.roll(top, 64, axis=1), bottom),
    )


def receiver_kernel(place, bad, rcv_ref, out_ref, held, turned):
    windows, chans, _ = rcv_ref.shape
    ids = place[1] * chans + lax.broadcasted_iota(jnp.int32, (chans, 128), 0)
    faulty = ids < 0
    for i in range(bad.shape[0]):
        faulty = faulty | (ids == bad[i])
    keep = jnp.where(faulty, 0.0, 1.0).astype(F32)[None, :, :1]
    group = 8

    @pl.loop(0, windows // group)
    def _(j):
        data = rcv_ref[pl.ds(j * group, group)].astype(F32)
        parts = whiten_parts(data[..., :HALF], data[..., HALF:], keep)
        rows = pl.ds(pl.multiple_of(j * group * chans, group * chans), group * chans)
        for q in range(4):
            for i in range(2):
                lanes = parts[i][..., q * 128 : q * 128 + 128]
                held[2 * q + i, rows, :] = lanes.reshape(group * chans, 128)

    @pl.loop(0, 4)
    def _(q):
        for c in range(0, chans, 2):
            pair = turn_pair(
                *(
                    held[2 * q + part, pl.ds(c + i, windows, stride=chans), :]
                    for i in range(2)
                    for part in range(2)
                )
            )
            for i in range(2):
                turned[pl.ds(q * 64 * chans + c + i, 64, stride=chans), :] = pair[i]

    @pl.loop(0, 4)
    def _(j):
        rows = turned[pl.ds(pl.multiple_of(j * 64 * chans, 64 * chans), 64 * chans), :]
        out_ref[pl.ds(j * 64, 64)] = rows.reshape(64, chans, 128).astype(BF16)


def receiver_blocks(rcv, place, bad):
    windows, chans, _ = rcv.shape
    return pl.pallas_call(
        receiver_kernel,
        out_shape=jax.ShapeDtypeStruct((256, chans, 128), BF16),
        grid_spec=pltpu.PrefetchScalarGridSpec(
            num_scalar_prefetch=2,
            grid=(1,),
            in_specs=[pl.BlockSpec(rcv.shape, lambda i, p, b: (0, 0, 0))],
            out_specs=pl.BlockSpec((256, chans, 128), lambda i, p, b: (0, 0, 0)),
            scratch_shapes=[
                pltpu.VMEM((8, windows * chans, 128), F32),
                pltpu.VMEM((256 * chans, 128), F32),
            ],
        ),
        compiler_params=pltpu.CompilerParams(vmem_limit_bytes=VMEM),
        cost_estimate=pl.CostEstimate(
            flops=20_000_000, bytes_accessed=2 * 2**20, transcendentals=300_000
        ),
    )(place, bad, rcv)


def take(away, pieces, core, target, sem):
    windows = target.shape[0]
    far_low, far_high, up, down, own = (ref.at[:, pl.ds(core * 64, 64)] for ref in pieces)

    def fetch(pairs):
        copies = [pltpu.make_async_copy(a, b, sem.at[i]) for i, (a, b) in enumerate(pairs)]
        for copy in copies:
            copy.start()
        for copy in copies:
            copy.wait()

    mid = windows // 2
    low, high = target.at[pl.ds(0, mid)], target.at[pl.ds(mid, mid)]
    for distance, pairs in (
        (0, [(own, target)]),
        (1, [(up, target)]),
        (2, [(far_low, low), (far_high, high)]),
        (3, [(down, target)]),
    ):
        pl.when(away == distance)(functools.partial(fetch, pairs))


def share_kernel(core, place, *refs):
    take(place[3], refs[:5], core, refs[5], refs[6])


def share(core, place, pieces):
    windows = pieces[-1].shape[0]
    return pl.pallas_call(
        functools.partial(share_kernel, core),
        out_shape=jax.ShapeDtypeStruct((windows, 64, 256), BF16),
        grid_spec=pltpu.PrefetchScalarGridSpec(
            num_scalar_prefetch=1,
            grid=(1,),
            in_specs=[pl.BlockSpec(memory_space=pl.ANY)] * 5,
            out_specs=pl.BlockSpec((windows, 64, 256), lambda i, p: (0, 0, 0)),
            scratch_shapes=[pltpu.SemaphoreType.DMA((2,))],
        ),
        compiler_params=pltpu.CompilerParams(vmem_limit_bytes=VMEM // 2),
    )(place, *pieces)


def turn_kernel(holder_core, place, *refs):
    shared, out_ref, piece, held, turned, sem = refs[5:]
    windows = piece.shape[0]

    @pl.when(place[2] == holder_core)
    def _():
        take(place[3], refs[:5], holder_core, piece, sem)

    @pl.when(place[2] != holder_core)
    def _():
        copy = pltpu.make_async_copy(shared, piece, sem.at[0])
        copy.start()
        copy.wait()

    @pl.loop(0, windows // 4)
    def _(j):
        rows = pl.ds(pl.multiple_of(j * 256, 256), 256)
        for part in range(2):
            lanes = piece[pl.ds(j * 4, 4), :, part * 128 : part * 128 + 128]
            held[part, rows, :] = lanes.astype(F32).reshape(256, 128)

    @pl.loop(0, 8)
    def _(s):
        for w in range(0, 8, 2):
            pair = turn_pair(
                *(
                    held[part, pl.ds(w * 8 + i * 8 + s, windows, stride=64), :]
                    for i in range(2)
                    for part in range(2)
                )
            )
            for i in range(2):
                turned[pl.ds(s * 8 + w + i, 64, stride=64), :] = pair[i]

    @pl.loop(0, 8)
    def _(j):
        rows = turned[pl.ds(pl.multiple_of(j * 512, 512), 512), :]
        out_ref[pl.ds(j * 8, 8)] = rows.reshape(8, 64, 128).astype(BF16)


def turn_source(holder_core, place, pieces, shared):
    windows = pieces[-1].shape[0]
    return pl.pallas_call(
        functools.partial(turn_kernel, holder_core),
        out_shape=jax.ShapeDtypeStruct((64, 64, 128), BF16),
        grid_spec=pltpu.PrefetchScalarGridSpec(
            num_scalar_prefetch=1,
            grid=(1,),
            in_specs=[pl.BlockSpec(memory_space=pl.ANY)] * 6,
            out_specs=pl.BlockSpec((64, 64, 128), lambda i, p: (0, 0, 0)),
            scratch_shapes=[
                pltpu.VMEM((windows, 64, 256), BF16),
                pltpu.VMEM((2, windows * 64, 128), F32),
                pltpu.VMEM((64 * 64, 128), F32),
                pltpu.SemaphoreType.DMA((2,)),
            ],
        ),
        compiler_params=pltpu.CompilerParams(vmem_limit_bytes=VMEM // 2),
    )(place, *pieces, shared)


def cross_kernel(place, src_ref, rcv_ref, out_ref, left):
    row = lax.broadcasted_iota(jnp.int32, (512, 256), 0)
    col = lax.broadcasted_iota(jnp.int32, (512, 256), 1)
    wanted = ((row // 2) % 2) * 128 + (row % 2) * 64 + row // 8
    spread = (wanted == col).astype(F32).astype(BF16)
    lane = lax.broadcasted_iota(jnp.int32, (512, 128), 1)
    used = (lax.broadcasted_iota(jnp.int32, (512, 128), 0) // 4) % 2 == lane // 64
    is_real = lane[:128] % 64 < 32
    for win in range(8):
        plain = src_ref[win, 0]
        wide = plain.astype(F32)
        turned = jnp.where(is_real, -pltpu.roll(wide, 96, axis=1), pltpu.roll(wide, 32, axis=1))
        both = jnp.concatenate([plain, turned.astype(BF16)], axis=0)
        rows = jnp.dot(spread, both, preferred_element_type=F32)
        left[:, win * 128 : win * 128 + 128] = jnp.where(used, rows, 0.0).astype(BF16)
    group = lax.broadcasted_iota(jnp.int32, (64, 128), 1) // 16
    for x in range(4):
        right = jnp.concatenate([rcv_ref[x * 8 + win] for win in range(8)], axis=1)
        sums = lax.dot_general(
            left[...], right, (((1,), (1,)), ((), ())), preferred_element_type=F32
        )
        held = [sums[s * 64 : s * 64 + 64] for s in range(8)]
        for bit in (4, 2, 1):
            low = (group & bit) == 0
            for s in range(8):
                if s & bit:
                    continue
                a, b = held[s], held[s + bit]
                held[s] = jnp.where(low, a, pltpu.roll(b, 16 * bit, axis=1))
                held[s + bit] = jnp.where(low, pltpu.roll(a, 128 - 16 * bit, axis=1), b)
        for g in range(8):
            first = x * 64 + g * 8
            out_ref[first : first + 8] = held[g].reshape(8, 8, 128).astype(BF16)


def cross_sums(place, src, rcv):
    return pl.pallas_call(
        cross_kernel,
        out_shape=jax.ShapeDtypeStruct((256, 8, 128), BF16),
        grid_spec=pltpu.PrefetchScalarGridSpec(
            num_scalar_prefetch=1,
            grid=(1,),
            in_specs=[
                pl.BlockSpec((8, 1, 128, 128), lambda i, p: (0, p[4], 0, 0)),
                pl.BlockSpec(rcv.shape, lambda i, p: (0, 0, 0)),
            ],
            out_specs=pl.BlockSpec((256, 8, 128), lambda i, p: (0, 0, 0)),
            scratch_shapes=[pltpu.VMEM((512, 1024), BF16)],
        ),
        compiler_params=pltpu.CompilerParams(vmem_limit_bytes=VMEM // 2),
    )(place, src.reshape(8, 4, 128, 128), rcv)


def lag_kernel(cross_ref, high_ref, low_ref, out_ref, wide, sums):
    @pl.when(pl.program_id(0) == 0)
    def _():
        wide[...] = cross_ref[...].astype(F32).reshape(2048, 128)
        for b in range(8):
            rows, cols = b % 2 * 128, b // 2 * 256
            sums[rows : rows + 128, cols : cols + 256] = (
                wide[pl.ds(b, 256, stride=8), :].T.astype(BF16)
            )

    out_ref[...] = jnp.dot(sums[...], high_ref[...], preferred_element_type=F32) + jnp.dot(
        sums[...], low_ref[...], preferred_element_type=F32
    )


def to_lags(cross, high, low):
    return pl.pallas_call(
        lag_kernel,
        out_shape=jax.ShapeDtypeStruct((256, LAGS), F32),
        grid=(2,),
        in_specs=[
            pl.BlockSpec((256, 8, 128), lambda i: (0, 0, 0)),
            pl.BlockSpec((1024, 512), lambda i: (0, i)),
            pl.BlockSpec((1024, 512), lambda i: (0, i)),
        ],
        out_specs=pl.BlockSpec((256, 512), lambda i: (0, i)),
        scratch_shapes=[pltpu.VMEM((2048, 128), F32), pltpu.VMEM((256, 1024), BF16)],
        compiler_params=pltpu.CompilerParams(vmem_limit_bytes=VMEM),
    )(cross, high, low)


def inverse_table():
    x, zh, core, win = np.meshgrid(
        np.arange(4), np.arange(4), np.arange(2), np.arange(8), indexing="ij"
    )
    place = (x * 128 + (win * 4 + zh) * 2 + core).reshape(-1)
    lag = np.arange(LAGS)
    rows = []
    for j in range(2):
        freq = place + 64 * j
        phase = (freq[:, None] * lag[None, :] % LAGS) * (2.0 * math.pi / LAGS)
        weight = np.where(freq == 0, 1.0, 2.0)[:, None] / math.sqrt(WINDOWS * LAGS)
        rows += [weight * np.cos(phase), -weight * np.sin(phase)]
    table = np.concatenate(rows, axis=0).astype(np.float32)
    high = table.astype(BF16)
    low = (table - high.astype(np.float32)).astype(BF16)
    return jnp.asarray(high), jnp.asarray(low)


def exchange(x, core, pieces, receiver_spectra, bad_channels, place):
    far_low, far_high, up, down, own = pieces

    def hop(piece, start, step):
        pair = (start % 4 * 2 + core, (start + step) % 4 * 2 + core)
        return lax.ppermute(piece, ("x", "core"), [pair])

    far_low, far_high = hop(far_low, x, 1), hop(far_high, x, -1)
    up, down = hop(up, x, 1), hop(down, x, -1)
    blocks = receiver_blocks(receiver_spectra, place, bad_channels)
    rcv_at = lax.all_to_all(blocks, ("x", "y", "zl", "zh", "core"), 0, 0, tiled=True)
    far_low, far_high, _ = lax.optimization_barrier((far_low, far_high, blocks))
    far_low, far_high = hop(far_low, x + 1, 1), hop(far_high, x - 1, -1)
    pieces = (far_low, far_high, up, down, own)
    other = 1 - core
    shared = lax.ppermute(share(other, place, pieces), "core", [(core, other)])
    return turn_source(core, place, pieces, shared), rcv_at


def on_device(source_spectra, receiver_spectra, source_block, bad_channels):
    x, zh, core = (lax.axis_index(a) for a in ("x", "zh", "core"))
    holder = source_block[0]
    place = jnp.stack(
        [x, (x * 4 + zh) * 2 + core, core, (x - holder // 8) % 4, (holder // 2) % 4]
    ).astype(jnp.int32)
    src_blocks, rcv_at = lax.switch(
        holder // 8 * 2 + holder % 2,
        [functools.partial(exchange, i // 2, i % 2) for i in range(8)],
        tuple(source_pieces(source_spectra, place)),
        receiver_spectra,
        bad_channels,
        place,
    )
    src_at = lax.all_to_all(src_blocks, ("y", "zl", "zh", "core"), 0, 0, tiled=True)
    sums = cross_sums(place, src_at, rcv_at.reshape(32, 128, 128))
    mine = lax.all_to_all(sums, ("x", "zh", "core", "y", "zl"), 0, 0, tiled=True)
    high, low = inverse_table()
    return to_lags(mine, high, low).reshape(16, 16, LAGS)


def solution(mesh):
    fine = Mesh(mesh.devices.reshape(SIZES), AXES)
    win, rcv = AXES[:2], AXES[2:]
    return jax.shard_map(
        on_device,
        mesh=fine,
        in_specs=(P(win, rcv, None), P(win, rcv, None), P(), P()),
        out_specs=P(win, rcv, None),
        check_vma=False,
    )
```

```python
import functools
import math

import jax
import jax.numpy as jnp
import numpy as np
from jax import lax
from jax.experimental import pallas as pl
from jax.experimental.pallas import tpu as pltpu
from jax.sharding import Mesh
from jax.sharding import PartitionSpec as P

AXES = ("y", "zl", "x", "zh", "core")
SIZES = (4, 2, 4, 4, 2)
LAGS = 1024
HALF = 512
WINDOWS = 256
VMEM = 60 * 1024 * 1024
BF16 = jnp.bfloat16
F32 = jnp.float32


def whiten_parts(re, im, keep=None):
    power = re * re + im * im
    level = jnp.mean(power, axis=-1, keepdims=True)
    factor = lax.rsqrt(power + 0.1 * level + 1e-06)
    if keep is not None:
        factor = factor * keep
    return re * factor, im * factor


def source_kernel(place, src_ref, far_low, far_high, up, down, own):
    step, steps = pl.program_id(0), pl.num_programs(0)

    def part(start):
        return src_ref[:, :, pl.ds(start, 128)].astype(F32)

    total = None
    for q in range(4):
        re, im = part(q * 128), part(HALF + q * 128)
        power = re * re + im * im
        total = power if total is None else total + power
    level = 0.1 * (jnp.sum(total, axis=-1, keepdims=True) / HALF) + 1e-06

    def emit(ahead, out):
        start = lax.rem(place[0] + ahead, 4) * 128
        re = part(pl.multiple_of(start, 128))
        im = part(pl.multiple_of(HALF + start, 128))
        factor = lax.rsqrt(re * re + im * im + level)
        for i, value in enumerate((re * factor, im * factor)):
            rows = [
                value[:, w * 16 + k * 8 : w * 16 + k * 8 + 8] for k in range(2) for w in range(8)
            ]
            out[:, :, i * 128 : i * 128 + 128] = jnp.concatenate(rows, axis=1).astype(BF16)

    emit(0, own)
    emit(1, up)
    emit(3, down)
    pl.when(step < steps // 2)(functools.partial(emit, 2, far_low))
    pl.when(step >= steps // 2)(functools.partial(emit, 2, far_high))


def source_pieces(src, place):
    windows, sources, _ = src.shape
    block = 8
    steps = windows // block
    part = jax.ShapeDtypeStruct((windows // 2, sources, 256), BF16)
    piece = jax.ShapeDtypeStruct((windows, sources, 256), BF16)
    shape = (block, sources, 256)
    low = pl.BlockSpec(shape, lambda i, p: (jnp.minimum(i, steps // 2 - 1), 0, 0))
    high = pl.BlockSpec(shape, lambda i, p: (jnp.maximum(i - steps // 2, 0), 0, 0))
    plain = pl.BlockSpec(shape, lambda i, p: (i, 0, 0))
    return pl.pallas_call(
        source_kernel,
        out_shape=[part] * 2 + [piece] * 3,
        grid_spec=pltpu.PrefetchScalarGridSpec(
            num_scalar_prefetch=1,
            grid=(steps,),
            in_specs=[pl.BlockSpec((block, sources, LAGS), lambda i, p: (i, 0, 0))],
            out_specs=[low, high] + [plain] * 3,
        ),
        compiler_params=pltpu.CompilerParams(vmem_limit_bytes=VMEM),
        cost_estimate=pl.CostEstimate(
            flops=40_000_000, bytes_accessed=16 * 2**20, transcendentals=2_000_000
        ),
    )(place, src)


def turn_pair(*parts):
    tall = jnp.concatenate(parts, axis=0).T
    low = lax.broadcasted_iota(jnp.int32, (64, 128), 1) < 64
    top, bottom = tall[:64], tall[64:]
    return (
        jnp.where(low, top, pltpu.roll(bottom, 64, axis=1)),
        jnp.where(low, pltpu.roll(top, 64, axis=1), bottom),
    )


def receiver_kernel(place, bad, rcv_ref, out_ref, held, turned):
    windows, chans, _ = rcv_ref.shape
    ids = place[1] * chans + lax.broadcasted_iota(jnp.int32, (chans, 128), 0)
    faulty = ids < 0
    for i in range(bad.shape[0]):
        faulty = faulty | (ids == bad[i])
    keep = jnp.where(faulty, 0.0, 1.0).astype(F32)[None, :, :1]
    group = 8

    @pl.loop(0, windows // group)
    def _(j):
        data = rcv_ref[pl.ds(j * group, group)].astype(F32)
        parts = whiten_parts(data[..., :HALF], data[..., HALF:], keep)
        rows = pl.ds(pl.multiple_of(j * group * chans, group * chans), group * chans)
        for q in range(4):
            for i in range(2):
                lanes = parts[i][..., q * 128 : q * 128 + 128]
                held[2 * q + i, rows, :] = lanes.reshape(group * chans, 128)

    @pl.loop(0, 2)
    def _(half):
        for q, c in ((half * 2 + i, c) for i in range(2) for c in range(0, chans, 2)):
            pair = turn_pair(
                *(
                    held[2 * q + part, pl.ds(c + i, windows, stride=chans), :]
                    for i in range(2)
                    for part in range(2)
                )
            )
            for i in range(2):
                turned[pl.ds(q * 64 * chans + c + i, 64, stride=chans), :] = pair[i]

    @pl.loop(0, 4)
    def _(j):
        rows = turned[pl.ds(pl.multiple_of(j * 64 * chans, 64 * chans), 64 * chans), :]
        out_ref[pl.ds(j * 64, 64)] = rows.reshape(64, chans, 128).astype(BF16)


def receiver_blocks(rcv, place, bad):
    windows, chans, _ = rcv.shape
    return pl.pallas_call(
        receiver_kernel,
        out_shape=jax.ShapeDtypeStruct((256, chans, 128), BF16),
        grid_spec=pltpu.PrefetchScalarGridSpec(
            num_scalar_prefetch=2,
            grid=(1,),
            in_specs=[pl.BlockSpec(rcv.shape, lambda i, p, b: (0, 0, 0))],
            out_specs=pl.BlockSpec((256, chans, 128), lambda i, p, b: (0, 0, 0)),
            scratch_shapes=[
                pltpu.VMEM((8, windows * chans, 128), F32),
                pltpu.VMEM((256 * chans, 128), F32),
            ],
        ),
        compiler_params=pltpu.CompilerParams(vmem_limit_bytes=VMEM),
        cost_estimate=pl.CostEstimate(
            flops=20_000_000, bytes_accessed=2 * 2**20, transcendentals=300_000
        ),
    )(place, bad, rcv)


def take(away, pieces, core, target, sem):
    windows = target.shape[0]
    far_low, far_high, up, down, own = (ref.at[:, pl.ds(core * 64, 64)] for ref in pieces)

    def fetch(pairs):
        copies = [pltpu.make_async_copy(a, b, sem.at[i]) for i, (a, b) in enumerate(pairs)]
        for copy in copies:
            copy.start()
        for copy in copies:
            copy.wait()

    mid = windows // 2
    low, high = target.at[pl.ds(0, mid)], target.at[pl.ds(mid, mid)]
    for distance, pairs in (
        (0, [(own, target)]),
        (1, [(up, target)]),
        (2, [(far_low, low), (far_high, high)]),
        (3, [(down, target)]),
    ):
        pl.when(away == distance)(functools.partial(fetch, pairs))


def share_kernel(core, place, *refs):
    take(place[3], refs[:5], core, refs[5], refs[6])


def share(core, place, pieces):
    windows = pieces[-1].shape[0]
    return pl.pallas_call(
        functools.partial(share_kernel, core),
        out_shape=jax.ShapeDtypeStruct((windows, 64, 256), BF16),
        grid_spec=pltpu.PrefetchScalarGridSpec(
            num_scalar_prefetch=1,
            grid=(1,),
            in_specs=[pl.BlockSpec(memory_space=pl.ANY)] * 5,
            out_specs=pl.BlockSpec((windows, 64, 256), lambda i, p: (0, 0, 0)),
            scratch_shapes=[pltpu.SemaphoreType.DMA((2,))],
        ),
        compiler_params=pltpu.CompilerParams(vmem_limit_bytes=VMEM // 2),
    )(place, *pieces)


def turn_kernel(holder_core, place, *refs):
    shared, out_ref, piece, held, turned, sem = refs[5:]
    windows = piece.shape[0]

    @pl.when(place[2] == holder_core)
    def _():
        take(place[3], refs[:5], holder_core, piece, sem)

    @pl.when(place[2] != holder_core)
    def _():
        copy = pltpu.make_async_copy(shared, piece, sem.at[0])
        copy.start()
        copy.wait()

    @pl.loop(0, windows // 4)
    def _(j):
        rows = pl.ds(pl.multiple_of(j * 256, 256), 256)
        for part in range(2):
            lanes = piece[pl.ds(j * 4, 4), :, part * 128 : part * 128 + 128]
            held[part, rows, :] = lanes.astype(F32).reshape(256, 128)

    @pl.loop(0, 8)
    def _(s):
        for w in range(0, 8, 2):
            pair = turn_pair(
                *(
                    held[part, pl.ds(w * 8 + i * 8 + s, windows, stride=64), :]
                    for i in range(2)
                    for part in range(2)
                )
            )
            for i in range(2):
                turned[pl.ds(s * 8 + w + i, 64, stride=64), :] = pair[i]

    @pl.loop(0, 8)
    def _(j):
        rows = turned[pl.ds(pl.multiple_of(j * 512, 512), 512), :]
        out_ref[pl.ds(j * 8, 8)] = rows.reshape(8, 64, 128).astype(BF16)


def turn_source(holder_core, place, pieces, shared):
    windows = pieces[-1].shape[0]
    return pl.pallas_call(
        functools.partial(turn_kernel, holder_core),
        out_shape=jax.ShapeDtypeStruct((64, 64, 128), BF16),
        grid_spec=pltpu.PrefetchScalarGridSpec(
            num_scalar_prefetch=1,
            grid=(1,),
            in_specs=[pl.BlockSpec(memory_space=pl.ANY)] * 6,
            out_specs=pl.BlockSpec((64, 64, 128), lambda i, p: (0, 0, 0)),
            scratch_shapes=[
                pltpu.VMEM((windows, 64, 256), BF16),
                pltpu.VMEM((2, windows * 64, 128), F32),
                pltpu.VMEM((64 * 64, 128), F32),
                pltpu.SemaphoreType.DMA((2,)),
            ],
        ),
        compiler_params=pltpu.CompilerParams(vmem_limit_bytes=VMEM // 2),
    )(place, *pieces, shared)


def cross_kernel(place, src_ref, rcv_ref, out_ref, left):
    row = lax.broadcasted_iota(jnp.int32, (512, 256), 0)
    col = lax.broadcasted_iota(jnp.int32, (512, 256), 1)
    wanted = ((row // 2) % 2) * 128 + (row % 2) * 64 + row // 8
    spread = (wanted == col).astype(F32).astype(BF16)
    lane = lax.broadcasted_iota(jnp.int32, (512, 128), 1)
    used = (lax.broadcasted_iota(jnp.int32, (512, 128), 0) // 4) % 2 == lane // 64
    is_real = lane[:128] % 64 < 32
    for win in range(8):
        plain = src_ref[win, 0]
        wide = plain.astype(F32)
        turned = jnp.where(is_real, -pltpu.roll(wide, 96, axis=1), pltpu.roll(wide, 32, axis=1))
        both = jnp.concatenate([plain, turned.astype(BF16)], axis=0)
        rows = jnp.dot(spread, both, preferred_element_type=F32)
        left[:, win * 128 : win * 128 + 128] = jnp.where(used, rows, 0.0).astype(BF16)
    group = lax.broadcasted_iota(jnp.int32, (64, 128), 1) // 16
    for x in range(4):
        right = jnp.concatenate([rcv_ref[x * 8 + win] for win in range(8)], axis=1)
        sums = lax.dot_general(
            left[...], right, (((1,), (1,)), ((), ())), preferred_element_type=F32
        )
        held = [sums[s * 64 : s * 64 + 64] for s in range(8)]
        for bit in (4, 2, 1):
            low = (group & bit) == 0
            for s in range(8):
                if s & bit:
                    continue
                a, b = held[s], held[s + bit]
                held[s] = jnp.where(low, a, pltpu.roll(b, 16 * bit, axis=1))
                held[s + bit] = jnp.where(low, pltpu.roll(a, 128 - 16 * bit, axis=1), b)
        for g in range(8):
            first = x * 64 + g * 8
            out_ref[first : first + 8] = held[g].reshape(8, 8, 128).astype(BF16)


def cross_sums(place, src, rcv):
    return pl.pallas_call(
        cross_kernel,
        out_shape=jax.ShapeDtypeStruct((256, 8, 128), BF16),
        grid_spec=pltpu.PrefetchScalarGridSpec(
            num_scalar_prefetch=1,
            grid=(1,),
            in_specs=[
                pl.BlockSpec((8, 1, 128, 128), lambda i, p: (0, p[4], 0, 0)),
                pl.BlockSpec(rcv.shape, lambda i, p: (0, 0, 0)),
            ],
            out_specs=pl.BlockSpec((256, 8, 128), lambda i, p: (0, 0, 0)),
            scratch_shapes=[pltpu.VMEM((512, 1024), BF16)],
        ),
        compiler_params=pltpu.CompilerParams(vmem_limit_bytes=VMEM // 2),
    )(place, src.reshape(8, 4, 128, 128), rcv)


def lag_kernel(cross_ref, high_ref, low_ref, out_ref, wide, sums):
    @pl.when(pl.program_id(0) == 0)
    def _():
        wide[...] = cross_ref[...].astype(F32).reshape(2048, 128)
        for b in range(8):
            rows, cols = b % 2 * 128, b // 2 * 256
            sums[rows : rows + 128, cols : cols + 256] = (
                wide[pl.ds(b, 256, stride=8), :].T.astype(BF16)
            )

    out_ref[...] = jnp.dot(sums[...], high_ref[...], preferred_element_type=F32) + jnp.dot(
        sums[...], low_ref[...], preferred_element_type=F32
    )


def to_lags(cross, high, low):
    return pl.pallas_call(
        lag_kernel,
        out_shape=jax.ShapeDtypeStruct((256, LAGS), F32),
        grid=(2,),
        in_specs=[
            pl.BlockSpec((256, 8, 128), lambda i: (0, 0, 0)),
            pl.BlockSpec((1024, 512), lambda i: (0, i)),
            pl.BlockSpec((1024, 512), lambda i: (0, i)),
        ],
        out_specs=pl.BlockSpec((256, 512), lambda i: (0, i)),
        scratch_shapes=[pltpu.VMEM((2048, 128), F32), pltpu.VMEM((256, 1024), BF16)],
        compiler_params=pltpu.CompilerParams(vmem_limit_bytes=VMEM),
    )(cross, high, low)


def inverse_table():
    x, zh, core, win = np.meshgrid(
        np.arange(4), np.arange(4), np.arange(2), np.arange(8), indexing="ij"
    )
    place = (x * 128 + (win * 4 + zh) * 2 + core).reshape(-1)
    lag = np.arange(LAGS)
    rows = []
    for j in range(2):
        freq = place + 64 * j
        phase = (freq[:, None] * lag[None, :] % LAGS) * (2.0 * math.pi / LAGS)
        weight = np.where(freq == 0, 1.0, 2.0)[:, None] / math.sqrt(WINDOWS * LAGS)
        rows += [weight * np.cos(phase), -weight * np.sin(phase)]
    table = np.concatenate(rows, axis=0).astype(np.float32)
    high = table.astype(BF16)
    low = (table - high.astype(np.float32)).astype(BF16)
    return jnp.asarray(high), jnp.asarray(low)


def exchange(x, core, pieces, receiver_spectra, bad_channels, place):
    far_low, far_high, up, down, own = pieces

    def hop(piece, start, step):
        pair = (start % 4 * 2 + core, (start + step) % 4 * 2 + core)
        return lax.ppermute(piece, ("x", "core"), [pair])

    far_low, far_high = hop(far_low, x, 1), hop(far_high, x, -1)
    up, down = hop(up, x, 1), hop(down, x, -1)
    blocks = receiver_blocks(receiver_spectra, place, bad_channels)
    rcv_at = lax.all_to_all(blocks, ("x", "y", "zl", "zh", "core"), 0, 0, tiled=True)
    far_low, far_high, _ = lax.optimization_barrier((far_low, far_high, blocks))
    far_low, far_high = hop(far_low, x + 1, 1), hop(far_high, x - 1, -1)
    pieces = (far_low, far_high, up, down, own)
    other = 1 - core
    shared = lax.ppermute(share(other, place, pieces), "core", [(core, other)])
    return turn_source(core, place, pieces, shared), rcv_at


def on_device(source_spectra, receiver_spectra, source_block, bad_channels):
    x, zh, core = (lax.axis_index(a) for a in ("x", "zh", "core"))
    holder = source_block[0]
    place = jnp.stack(
        [x, (x * 4 + zh) * 2 + core, core, (x - holder // 8) % 4, (holder // 2) % 4]
    ).astype(jnp.int32)
    src_blocks, rcv_at = lax.switch(
        holder // 8 * 2 + holder % 2,
        [functools.partial(exchange, i // 2, i % 2) for i in range(8)],
        tuple(source_pieces(source_spectra, place)),
        receiver_spectra,
        bad_channels,
        place,
    )
    src_at = lax.all_to_all(src_blocks, ("y", "zl", "zh", "core"), 0, 0, tiled=True)
    sums = cross_sums(place, src_at, rcv_at.reshape(32, 128, 128))
    mine = lax.all_to_all(sums, ("x", "zh", "core", "y", "zl"), 0, 0, tiled=True)
    high, low = inverse_table()
    return to_lags(mine, high, low).reshape(16, 16, LAGS)


def solution(mesh):
    fine = Mesh(mesh.devices.reshape(SIZES), AXES)
    win, rcv = AXES[:2], AXES[2:]
    return jax.shard_map(
        on_device,
        mesh=fine,
        in_specs=(P(win, rcv, None), P(win, rcv, None), P(), P()),
        out_specs=P(win, rcv, None),
        check_vma=False,
    )
```
